32 devices in a mesh: groups: 2 (over y), gx: 4 (over z), gy: 2 (over x), gz: 2 (over core).
Axes of the slice: x: 2, y: 2, z: 4, core: 2. Of those that a mesh axis runs over, the one named last changes fastest.
Arguments:
- node_feats: bfloat16 [4096, 128], P(('groups', 'gx', 'gy', 'gz')), parts along dimension 0, may hold values from -6 to 6
- species: int32 [4096], P(('groups', 'gx', 'gy', 'gz')), parts along dimension 0, may hold values from 0 to 7
- export_index: int32 [512], P(('groups', 'gx', 'gy', 'gz')), parts along dimension 0, may hold values from 0 to 127
- pair_first: int32 [32768], P(('groups', 'gx', 'gy', 'gz')), parts along dimension 0, may hold values from 0 to 127, as said below
- pair_second: int32 [32768], P(('groups', 'gx', 'gy', 'gz')), parts along dimension 0, may hold values from 0 to 559, as said below
- pair_live: int32 [32768], P(('groups', 'gx', 'gy', 'gz')), parts along dimension 0, may hold values 0 or 1
- displacement: float32 [3, 32768], P(None, ('groups', 'gx', 'gy', 'gz')), parts along dimension 1, may hold values from -2.8 to 2.8, as said below
- w_up: bfloat16 [128, 128], replicated, may hold values from -0.5 to 0.5
- radial_one: float32 [8, 64], replicated, may hold values from -2 to 2
- radial_two: float32 [64, 64], replicated, may hold values from -0.75 to 0.75
- radial_three: float32 [64, 384], replicated, may hold values from -0.75 to 0.75
- power_weight: float32 [3, 128], replicated, may hold values from 0.2 to 1
- w_mix: bfloat16 [128, 128], replicated, may hold values from -0.5 to 0.5
- read_table: float32 [8, 128], replicated, may hold values from -0.5 to 0.5
- base_energy: float32 [8], replicated, may hold values from -3 to -1
Outputs:
- atom_energy: float32 [4096], P(('groups', 'gx', 'gy', 'gz')), parts along dimension 0
- pair_forces: float32 [3, 4096], P(None, ('groups', 'gx', 'gy', 'gz')), parts along dimension 1
- feats_grad: bfloat16 [4096, 128], P(('groups', 'gx', 'gy', 'gz')), parts along dimension 0
The draws below stay inside these ranges and needn't reach their ends.
There are 2 independent parts, one for each index of `groups`. The reference program is written for one: setup_inputs(seed, part) draws one part's arguments, and reference() takes and returns one part's arrays. A program takes and returns all parts, laid end to end along the dimension named above; an argument that names none is the same for every part. Nothing has to cross between parts.
Inputs may be any that keep to these rules, and one draw needn't show every extreme that they name: `export_index`: entries may repeat. `pair_first`: A local row of the pair's domain. `pair_second`: A domain's pair slots h < 592 and its slots 1024 - 27 * 16 + 13 * 16 + r (r < 16) name a local row below 128 other than the pair's first atom; its slot 592 + g * 16 + r with g != 13 names 128 + g * 16 + e for some e below 16, a ghost slot of block g = 9 a + 3 b + c. `displacement`: each component's magnitude is at least 0.8.
All inputs are finite; a program needn't handle non-finite values. No bound on the sum of `pair_live` on one device may be relied on, other than what follows from the above.
Results may differ from the reference program's by a relative error of at most 0.0061.
Values may be sent and summed in bfloat16 or wider, within the bound.
A program may use at most 64 MiB of HBM per device.

```python
import math
import jax
import jax.numpy as jnp
from jax import lax

C = 128
RH = 64
RB = 8
SPECIES = 8
ATOM_DEV = 128
EXPORT = 16
REMOTE = 16
PAIRS_DEV = 1024
ATOMS = 2048
EXPORTS = 256
PAIRS = 16384
N_GX = 4
N_GY = 2
N_GZ = 2


def pair_rows(key):
    keys = jax.random.split(key, 3)
    first_atom = jax.random.randint(keys[0], (PAIRS,), 0, ATOM_DEV)
    slot_index = jax.random.randint(keys[1], (PAIRS,), 0, EXPORT)
    offset = jax.random.randint(keys[2], (PAIRS,), 1, ATOM_DEV)
    position = jnp.arange(PAIRS) % PAIRS_DEV
    head_count = PAIRS_DEV - 27 * REMOTE
    block_index = jnp.maximum(position - head_count, 0) // REMOTE
    remote = (position >= head_count) & (block_index != 13)
    local_second = (first_atom + offset) % ATOM_DEV
    second_atom = jnp.where(remote, ATOM_DEV + block_index * EXPORT + slot_index, local_second)
    first_atom = jnp.where(position == 0, ATOM_DEV - 1, first_atom)
    second_atom = jnp.where(position == 0, 0, second_atom)
    second_atom = jnp.where(position == PAIRS_DEV - 1, ATOM_DEV + 27 * EXPORT - 1, second_atom)
    return (first_atom.astype(jnp.int32), second_atom.astype(jnp.int32))


def draw_pair_first(key, part):
    return pair_rows(key)[0]


def draw_pair_second(key, part):
    return pair_rows(key)[1]


def draw_displacement(key, part):
    key = jax.random.fold_in(key, 7)
    keys = jax.random.split(key, 2)
    magnitude = jax.random.uniform(keys[0], (3, PAIRS), dtype=jnp.float32, minval=0.8, maxval=2.8)
    sign_flip = 2.0 * jax.random.randint(keys[1], (3, PAIRS), 0, 2).astype(jnp.float32) - 1.0
    return (sign_flip * magnitude).astype(jnp.float32)


def with_ends(entries, own_key, low, high):
    longest = entries.shape.index(max(entries.shape))
    spots = []
    for shift in (0, 1):
        where = [jax.random.randint(jax.random.fold_in(own_key, axis), (), 0, length) for axis, length in enumerate(entries.shape)]
        where[longest] = (where[longest] + shift) % entries.shape[longest]
        spots.append(tuple(where))
    return entries.at[spots[0]].set(low).at[spots[1]].set(high)


def steps_of(stream_key, dims, cuts, least, top_value):
    def one(dim, blocks):
        draws = jax.random.uniform(jax.random.fold_in(jax.random.fold_in(stream_key, 6), dim), (blocks,), jnp.float32, least / len(cuts), top_value / len(cuts))
        return jnp.repeat(jnp.exp(draws), dims[dim] // blocks).reshape((-1,) + (1,) * (len(dims) - dim - 1))

    factor_of = one(*cuts[0])
    for cut in cuts[1:]:
        factor_of = factor_of * one(*cut)
    return factor_of


def normal_values(key, dims, scale, limit, shards=(), kind=jnp.bfloat16):
    gain = steps_of(key, dims, shards, -0.22, 0.18) if shards else 1.0
    array = jax.random.normal(key, dims, jnp.float32) * scale * gain
    return jnp.minimum(jnp.maximum(array, -limit), limit).astype(kind)


def setup_inputs(seed: int = 0, part: int = 0) -> dict:
    streams_of = jax.random.split(jax.random.key(seed), 16)
    own_keys = jax.random.split(jax.random.fold_in(streams_of[15], part), 16)
    return {
        "node_feats": normal_values(own_keys[0], (ATOMS, C), 1.0, 6.0, ((0, 16),)),
        "species": with_ends(jax.random.randint(own_keys[1], (ATOMS,), 0, SPECIES), jax.random.fold_in(own_keys[1], 1), 0, SPECIES - 1).astype(jnp.int32),
        "export_index": with_ends(jax.random.randint(own_keys[2], (EXPORTS,), 0, ATOM_DEV), jax.random.fold_in(own_keys[2], 1), 0, ATOM_DEV - 1).astype(jnp.int32),
        "pair_first": draw_pair_first(jax.random.fold_in(jax.random.fold_in(streams_of[15], part), 71), part),
        "pair_second": draw_pair_second(jax.random.fold_in(jax.random.fold_in(streams_of[15], part), 71), part),
        "pair_live": with_ends((jax.random.randint(own_keys[5], (PAIRS,), 0, 8) < 7).astype(jnp.int32), jax.random.fold_in(own_keys[5], 1), 0, 1),
        "displacement": draw_displacement(jax.random.fold_in(jax.random.fold_in(streams_of[15], part), 71), part),
        "w_up": normal_values(streams_of[7], (C, C), C ** -0.5, 0.5),
        "radial_one": normal_values(streams_of[8], (RB, RH), RB ** -0.5, 2.0, (), jnp.float32),
        "radial_two": normal_values(streams_of[9], (RH, RH), RH ** -0.5, 0.75, (), jnp.float32),
        "radial_three": normal_values(streams_of[10], (RH, 3 * C), RH ** -0.5, 0.75, (), jnp.float32),
        "power_weight": jnp.clip(jax.random.uniform(streams_of[11], (3, C), jnp.float32, 0.2, 1.0), 0.2, 1.0),
        "w_mix": normal_values(streams_of[12], (C, C), C ** -0.5, 0.5),
        "read_table": normal_values(streams_of[13], (SPECIES, C), C ** -0.5, 0.5, (), jnp.float32),
        "base_energy": jnp.clip(jax.random.uniform(streams_of[14], (SPECIES,), jnp.float32, -3.0, -1.0), -3.0, -1.0),
    }


PRECISE = lax.Precision.HIGHEST
CUTOFF = 5.0
ROOT_THREE = math.sqrt(3.0)
ROOT_FIVE = math.sqrt(5.0)
ROOT_FIFTEEN = math.sqrt(15.0)
PARITY_SIGNS = (1.0, -1.0, -1.0, -1.0, 1.0, 1.0, 1.0, 1.0, 1.0)

def harmonics(direction):
    along_x = direction[:, 0]
    along_y = direction[:, 1]
    along_z = direction[:, 2]
    constant = jnp.ones_like(along_x)
    return jnp.stack([constant, ROOT_THREE * along_x, ROOT_THREE * along_y, ROOT_THREE * along_z, ROOT_FIFTEEN * along_x * along_z, ROOT_FIFTEEN * along_x * along_y, ROOT_FIVE * (along_y * along_y - 0.5 * (along_x * along_x + along_z * along_z)), ROOT_FIFTEEN * along_y * along_z, 0.5 * ROOT_FIFTEEN * (along_z * along_z - along_x * along_x)], axis=1)

def geometry(vectors, radial_one, radial_two, radial_three):
    distance = jnp.sqrt(lax.optimization_barrier(jnp.sum(vectors * vectors, axis=1)))
    direction = vectors / distance[:, None]
    scaled = distance / CUTOFF
    orders = jnp.arange(1, radial_one.shape[0] + 1, dtype=jnp.float32)
    bessel = math.sqrt(2.0 / CUTOFF) * jnp.sin(math.pi * orders[None, :] * scaled[:, None]) / distance[:, None]
    envelope = 1.0 - 28.0 * scaled ** 6 + 48.0 * scaled ** 7 - 21.0 * scaled ** 8
    basis_rows = bessel * envelope[:, None]
    hidden_one = jax.nn.silu(jnp.dot(basis_rows, radial_one, precision=PRECISE))
    hidden_two = jax.nn.silu(jnp.dot(hidden_one, radial_two, precision=PRECISE))
    radial = jnp.dot(hidden_two, radial_three, precision=PRECISE)
    return (harmonics(direction), radial.reshape(vectors.shape[0], 3, -1))

def spread_degrees(values):
    return jnp.concatenate([values[:, 0:1], jnp.repeat(values[:, 1:2], 3, axis=1), jnp.repeat(values[:, 2:3], 5, axis=1)], axis=1)

def gather_degrees(values):
    return jnp.stack([values[:, 0], lax.optimization_barrier(jnp.sum(values[:, 1:4], axis=1)), lax.optimization_barrier(jnp.sum(values[:, 4:9], axis=1))], axis=1)

def pair_messages(vectors, first_up, second_up, weight, radial_one, radial_two, radial_three):
    harmonic, radial = geometry(vectors, radial_one, radial_two, radial_three)
    parity = jnp.asarray(PARITY_SIGNS, dtype=jnp.float32)
    spread = spread_degrees(radial) * weight[:, None, None]
    toward_first = spread * harmonic[:, :, None] * second_up[:, None, :]
    toward_second = spread * (harmonic * parity)[:, :, None] * first_up[:, None, :]
    return (toward_first, toward_second)

def pair_gradients(vectors, first_up, second_up, first_grad, second_grad, weight, radial_one, radial_two, radial_three):

    def shape_terms(moved_vectors):
        return geometry(moved_vectors, radial_one, radial_two, radial_three)
    (harmonic, radial), pullback = jax.vjp(shape_terms, vectors)
    parity = jnp.asarray(PARITY_SIGNS, dtype=jnp.float32)
    spread = spread_degrees(radial)
    lean_first = first_grad * harmonic[:, :, None]
    lean_second = second_grad * (harmonic * parity)[:, :, None]
    grad_spread = weight[:, None, None] * (lean_first * second_up[:, None, :] + lean_second * first_up[:, None, :])
    up_second = weight[:, None] * lax.optimization_barrier(jnp.sum(lean_first * spread, axis=1))
    up_first = weight[:, None] * lax.optimization_barrier(jnp.sum(lean_second * spread, axis=1))
    grad_harmonic = weight[:, None] * (lax.optimization_barrier(jnp.sum(first_grad * spread * second_up[:, None, :], axis=2)) + parity * lax.optimization_barrier(jnp.sum(second_grad * spread * first_up[:, None, :], axis=2)))
    grad_vectors, = pullback((grad_harmonic, gather_degrees(grad_spread)))
    return (up_first, up_second, grad_vectors)

def node_terms(amps, species, power_weight, w_mix, read_table, base_energy):
    squares = amps * amps
    product = (amps[:, 0] + power_weight[0] * squares[:, 0] + power_weight[1] * lax.optimization_barrier(jnp.sum(squares[:, 1:4], axis=1)) + power_weight[2] * lax.optimization_barrier(jnp.sum(squares[:, 4:9], axis=1))).astype(jnp.bfloat16)
    mixed_rows = jnp.dot(product, w_mix, preferred_element_type=jnp.float32)
    picker = (species[:, None] == jnp.arange(read_table.shape[0], dtype=jnp.int32)[None, :]).astype(jnp.float32)
    read_rows = jnp.dot(picker, read_table, precision=PRECISE)
    offsets = jnp.dot(picker, base_energy, precision=PRECISE)
    sigmoid = jax.nn.sigmoid(mixed_rows)
    energy = lax.optimization_barrier(jnp.sum(mixed_rows * sigmoid * read_rows, axis=1)) + offsets
    grad_mixed = (read_rows * sigmoid * (1.0 + mixed_rows * (1.0 - sigmoid))).astype(jnp.bfloat16)
    grad_product = jnp.dot(grad_mixed, w_mix.T, preferred_element_type=jnp.float32)
    first_hot = (jnp.arange(9, dtype=jnp.int32) == 0).astype(jnp.float32)
    power_spread = spread_degrees(power_weight[None])[0]
    grad_amps = (grad_product[:, None, :] * (first_hot[None, :, None] + 2.0 * power_spread[None] * amps)).astype(jnp.bfloat16)
    return (energy, grad_amps)

def reference(node_feats, species, export_index, pair_first, pair_second, pair_live, displacement, w_up, radial_one, radial_two, radial_three, power_weight, w_mix, read_table, base_energy):
    domains = N_GX * N_GY * N_GZ
    atom_count = ATOM_DEV
    slot_count = EXPORT
    pair_count = PAIRS_DEV
    channels = node_feats.shape[1]
    up_all = jnp.dot(node_feats, w_up, preferred_element_type=jnp.float32).astype(jnp.bfloat16)
    domain_ids = jnp.arange(domains, dtype=jnp.int32)
    exports = export_index.reshape(domains, slot_count).astype(jnp.int32) + domain_ids[:, None] * atom_count
    domain_x = domain_ids // (N_GY * N_GZ)
    domain_y = domain_ids // N_GZ % N_GY
    domain_z = domain_ids % N_GZ
    pieces = [domain_ids[:, None] * atom_count + jnp.arange(atom_count, dtype=jnp.int32)[None, :]]
    for offset_x in range(3):
        for offset_y in range(3):
            for offset_z in range(3):
                neighbor = ((domain_x + offset_x - 1) % N_GX * N_GY + (domain_y + offset_y - 1) % N_GY) * N_GZ + (domain_z + offset_z - 1) % N_GZ
                pieces.append(exports[neighbor])
    node_atom = jnp.concatenate(pieces, axis=1).astype(jnp.int32)
    first_global = pair_first.reshape(domains, pair_count).astype(jnp.int32) + domain_ids[:, None] * atom_count
    second_global = jnp.take_along_axis(node_atom, pair_second.reshape(domains, pair_count).astype(jnp.int32), axis=1)
    weight_all = (pair_live.astype(jnp.float32) / math.sqrt(2.0 * pair_count / atom_count)).reshape(domains, pair_count)
    vectors_all = displacement.T.reshape(domains, pair_count, 3)
    per_domain = (first_global, second_global, weight_all, vectors_all)

    def gather_step(amp_table, blocks):
        first_rows, second_rows, weight, vectors = blocks
        toward_first, toward_second = pair_messages(vectors, up_all[first_rows].astype(jnp.float32), up_all[second_rows].astype(jnp.float32), weight, radial_one, radial_two, radial_three)
        amp_table = amp_table.at[first_rows].add(toward_first).at[second_rows].add(toward_second)
        return (amp_table, None)
    amps, unused = lax.scan(gather_step, jnp.zeros((domains * atom_count, 9, channels), jnp.float32), per_domain)
    energy, grad_amps = node_terms(amps, species, power_weight, w_mix, read_table, base_energy)

    def grad_step(tables, blocks):
        up_table, force_table = tables
        first_rows, second_rows, weight, vectors = blocks
        up_first, up_second, grad_vectors = pair_gradients(vectors, up_all[first_rows].astype(jnp.float32), up_all[second_rows].astype(jnp.float32), grad_amps[first_rows].astype(jnp.float32), grad_amps[second_rows].astype(jnp.float32), weight, radial_one, radial_two, radial_three)
        up_table = up_table.at[first_rows].add(up_first).at[second_rows].add(up_second)
        force_table = force_table.at[first_rows].add(grad_vectors).at[second_rows].add(-grad_vectors)
        return ((up_table, force_table), None)
    start = (jnp.zeros((domains * atom_count, channels), jnp.float32), jnp.zeros((domains * atom_count, 3), jnp.float32))
    (up_grad, forces), unused = lax.scan(grad_step, start, per_domain)
    feats_grad = jnp.dot(up_grad.astype(jnp.bfloat16), w_up.T, preferred_element_type=jnp.float32).astype(jnp.bfloat16)
    return (energy, forces.T, feats_grad)
```

```python
import functools
import math

import jax
import jax.numpy as jnp
from jax import lax
from jax.experimental import pallas as pl
from jax.experimental.pallas import tpu as pltpu
from jax.sharding import PartitionSpec as P

CUTOFF = 5.0
S3 = math.sqrt(3.0)
S5 = math.sqrt(5.0)
S15 = math.sqrt(15.0)
F32 = jnp.float32
BF16 = jnp.bfloat16
MESH = pl.DeviceIdType.MESH
DEGREE_ROWS = ((0, 1), (1, 4), (4, 9))


def nn(a, b):
    return lax.dot_general(a, b, (((1,), (0,)), ((), ())), preferred_element_type=F32)


def nt(a, b):
    return lax.dot_general(a, b, (((1,), (1,)), ((), ())), preferred_element_type=F32)


def rounded(x):
    return x.astype(BF16).astype(F32)


def split_weights(w):
    depth, width = w.shape
    hi = rounded(w)
    stack = jnp.concatenate([hi, hi, w - hi], axis=0)
    rows = -(-3 * depth // 128) * 128
    stack = jnp.concatenate([stack, jnp.zeros((rows - 3 * depth, width), F32)], axis=0)
    columns = -(-width // 128) * 128
    if columns > width:
        stack = jnp.concatenate([stack, jnp.zeros((rows, columns - width), F32)], axis=1)
    return jnp.transpose(stack)[:width].astype(BF16)


def split_values(h, rows):
    hi = rounded(h)
    parts = [hi, h - hi, hi]
    spare = rows - 3 * h.shape[0]
    if spare:
        parts.append(jnp.zeros((spare, h.shape[1]), F32))
    return jnp.concatenate(parts, axis=0).astype(BF16)


def flipped(w):
    return jnp.transpose(w.astype(F32)).astype(BF16)


def polynomial(x, coefficients):
    total = coefficients[-1]
    for c in coefficients[-2::-1]:
        total = total * x + c
    return total


SIN_SERIES = [(-1.0) ** i / math.factorial(2 * i + 1) for i in range(7)]
COS_SERIES = [(-1.0) ** i / math.factorial(2 * i) for i in range(8)]


def direction(vx, vy, vz):
    square = vx * vx + vy * vy + vz * vz
    inverse = lax.rsqrt(square)
    return square * inverse, inverse, (vx * inverse, vy * inverse, vz * inverse)


def radial_network(distance, inverse, orders, one, two, three):
    lanes = distance.shape[1]
    x = distance * (1.0 / CUTOFF)
    phase = math.pi * x - 0.5 * math.pi
    square = phase * phase
    sine = polynomial(square, COS_SERIES)
    cosine = -phase * polynomial(square, SIN_SERIES)
    sines, cosines = [sine], [cosine]
    for _ in range(orders - 1):
        s, c = sines[-1], cosines[-1]
        sines.append(s * cosine + c * sine)
        cosines.append(c * cosine - s * sine)
    x2 = x * x
    x5 = x2 * x2 * x
    envelope = 1.0 - x5 * x * (28.0 - 48.0 * x + 21.0 * x2)
    slope = -168.0 * x5 * (1.0 - x) * (1.0 - x)
    scale = math.sqrt(2.0 / CUTOFF) * inverse
    factor = scale * envelope
    factor_slope = scale * (slope * (1.0 / CUTOFF) - envelope * inverse)
    sin_rows = jnp.concatenate(sines, axis=0)
    cos_rows = jnp.concatenate(cosines, axis=0)
    number = lax.broadcasted_iota(jnp.int32, (orders, lanes), 0).astype(F32) + 1.0
    basis = sin_rows * factor
    basis_slope = cos_rows * (number * (math.pi / CUTOFF)) * factor + sin_rows * factor_slope
    both = jnp.concatenate([basis, basis_slope], axis=1)
    for weights in (one, two):
        both = nn(weights, split_values(both, weights.shape[1]))
        value, tangent = both[:, :lanes], both[:, lanes:]
        sigmoid = jax.nn.sigmoid(value)
        hidden = value * sigmoid
        tangent = tangent * (sigmoid + hidden * (1.0 - sigmoid))
        both = jnp.concatenate([hidden, tangent], axis=1)
    both = nn(three, split_values(both, three.shape[1]))
    return both[:, :lanes], both[:, lanes:]


def harmonic_rows(n, w):
    x, y, z = n
    wx, wy, wz = (w * x, w * y, w * z)
    return (
        w,
        S3 * wx,
        S3 * wy,
        S3 * wz,
        S15 * wx * z,
        S15 * wx * y,
        S5 * (wy * y - 0.5 * (wx * x + wz * z)),
        S15 * wy * z,
        0.5 * S15 * (wz * z - wx * x),
    )


class Plan:
    def __init__(self, sizes, slots):
        self.sizes = sizes
        self.slots = slots
        self.classes = tuple(2 if n == 2 else 3 for n in sizes)
        self.subs = tuple(2 if n == 2 else 1 for n in sizes)
        self.count = math.prod(self.classes)
        self.members = [[] for _ in range(self.count)]
        self.sub_of = {}
        for g in range(27):
            o = (g // 9, g // 3 % 3, g % 3)
            index, sub = self.index(o), self.sub(o)
            self.members[index].append(g)
            self.sub_of[g] = sub
        self.own = self.index((1, 1, 1))
        self.others = [d for d in range(self.count) if d != self.own]
        self.start, self.rows, self.block_start = {}, {}, {}
        total = 0
        for d in self.others:
            self.start[d] = total
            self.rows[d] = slots * (2 + len(self.members[d]))
            for i, g in enumerate(self.members[d]):
                self.block_start[g] = total + slots * (2 + i)
            total += self.rows[d]
        self.total = total

    def index(self, o, turned=False):
        value = 0
        for part, n, classes in zip(o, self.sizes, self.classes):
            part = part & 1 if n == 2 else (2 - part if turned else part)
            value = value * classes + part
        return value

    def sub(self, o):
        value = 0
        for part, n, subs in zip(o, self.sizes, self.subs):
            value = value * subs + (part >> 1 if n == 2 else part * 0)
        return value

    def class_of_block(self, g):
        return self.index((g // 9, g // 3 % 3, g % 3))

    def shift(self, d):
        out = []
        for classes in reversed(self.classes):
            out.append(d % classes - 1)
            d //= classes
        return tuple(reversed(out))

    def lane_offsets(self, g):
        a = (g * 57) >> 9
        rest = g - 9 * a
        b = (rest * 11) >> 5
        return (a, b, rest - 3 * b)


def kernel(
    plan,
    feats_ref,
    species_ref,
    export_ref,
    first_ref,
    second_ref,
    live_ref,
    disp_ref,
    w_up_ref,
    one_ref,
    two_ref,
    three_ref,
    power_ref,
    w_mix_ref,
    read_ref,
    base_ref,
    energy_ref,
    force_ref,
    grad_ref,
    send_one,
    recv_one,
    send_two,
    recv_two,
    edge_in,
    info_in,
    ghost_in,
    radial_ref,
    slope_ref,
    up_ref,
    m_ref,
    s_ref,
    hot_one,
    hot_two,
    hot_back,
    hot_ghost,
    g_wide,
    g_tall,
    s1,
    r1,
    s2,
    r2,
):
    atoms, channels = feats_ref.shape
    pairs = first_ref.shape[1]
    slots = plan.slots
    head = pairs - 27 * slots
    cut = head // 128 * 128
    width = pairs - cut
    pad = head - cut
    orders = one_ref.shape[0]
    norm = 1.0 / math.sqrt(2.0 * pairs / atoms)

    me = tuple(lax.axis_index(a) for a in ("groups", "gx", "gy", "gz"))

    def device(d, turn):
        place = [me[0]]
        for here, step, n in zip(me[1:], plan.shift(d), plan.sizes):
            place.append(lax.rem(here + turn * step + n, n))
        return tuple(place)

    barrier = pltpu.get_barrier_semaphore()
    for d in plan.others:
        pl.semaphore_signal(barrier, inc=1, device_id=device(d, 1), device_id_type=MESH)

    lane = lax.broadcasted_iota(jnp.int32, (1, width), 1)
    block = jnp.maximum(lane - pad, 0) >> 4
    offsets = plan.lane_offsets(block)
    own_lane = jnp.logical_or(lane < pad, block == 13)
    lane_sub = plan.sub(offsets)
    ghost_base = plan.index(offsets, turned=True) * slots

    first = first_ref[...]
    second = second_ref[...]
    live = live_ref[...].astype(F32)
    vx, vy, vz = disp_ref[0:1, :], disp_ref[1:2, :], disp_ref[2:3, :]

    atom_row = lax.broadcasted_iota(jnp.int32, (atoms, pairs), 0)
    hot_one[...] = (atom_row == first).astype(F32).astype(BF16)
    hot_two[...] = (atom_row == second).astype(F32).astype(BF16)
    export_hot = (
        (lax.broadcasted_iota(jnp.int32, (atoms, slots), 0) == export_ref[...])
        .astype(F32)
        .astype(BF16)
    )
    feats = feats_ref[...]

    window_slot = (second[:, cut:] - atoms) & (slots - 1)
    rows16 = []
    for v in (vx, vy, vz):
        piece = v[:, cut:]
        for _ in range(3):
            hi = rounded(piece)
            rows16.append(hi)
            piece = piece - hi
    rows16.append(live[:, cut:])
    rows16.append(window_slot.astype(F32))
    rows16.append(jnp.zeros((16 - len(rows16), width), F32))
    group16 = jnp.concatenate(rows16, axis=0)
    tall_group = lax.broadcasted_iota(jnp.int32, (128, width), 0) >> 4
    tiled = jnp.concatenate([group16] * 8, axis=0)
    info_rows = jnp.transpose(jnp.where(tall_group == lane_sub, tiled, 0.0))

    def transposed_dot(a, b):
        return nn(jnp.transpose(a.astype(F32)).astype(BF16), b)

    first_rows = transposed_dot(hot_one[:, cut:], feats).astype(BF16)
    offered = transposed_dot(
        jnp.concatenate([export_hot.astype(F32), jnp.zeros((atoms, 128 - slots), F32)], axis=1),
        feats,
    )[:slots].astype(BF16)
    for d in plan.others:
        at = plan.start[d]
        send_one[at : at + slots, :] = offered
        tile = None
        for g in plan.members[d]:
            part = info_rows[pad + slots * g : pad + slots * (g + 1), :]
            tile = part if tile is None else tile + part
            spot = plan.block_start[g]
            send_one[spot : spot + slots, :] = first_rows[pad + slots * g : pad + slots * (g + 1), :]
        send_one[at + slots : at + 2 * slots, :] = tile.astype(BF16)

    pl.semaphore_wait(barrier, len(plan.others))
    first_copies = []
    for d in plan.others:
        part = pl.ds(plan.start[d], plan.rows[d])
        copy = pltpu.make_async_remote_copy(
            src_ref=send_one.at[part],
            dst_ref=recv_one.at[part],
            send_sem=s1.at[d],
            recv_sem=r1.at[d],
            device_id=device(d, 1),
            device_id_type=MESH,
        )
        copy.start()
        first_copies.append(copy)

    one = split_weights(one_ref[...])
    two = split_weights(two_ref[...])
    three = split_weights(three_ref[...])
    w_up = w_up_ref[...]
    w_up_t = flipped(w_up)
    w_mix = w_mix_ref[...]
    w_mix_t = flipped(w_mix)
    tables = jnp.transpose(
        jnp.concatenate(
            [
                power_ref[...],
                read_ref[...],
                jnp.zeros((128 - 3 - read_ref.shape[0], channels), F32),
            ],
            axis=0,
        )
    )
    up_t = nt(w_up_t, feats).astype(BF16)

    weight = live * norm
    edges = []

    def geometry(ax, ay, az, at):
        distance, inverse, n = direction(ax, ay, az)
        radial, slope = radial_network(distance, inverse, orders, one, two, three)
        lanes = ax.shape[1]
        radial_ref[:, at : at + lanes] = radial
        slope_ref[:, at : at + lanes] = slope
        return inverse, n

    def scaled_hot(hot, rows, at):
        hot = hot.astype(F32)
        lanes = hot.shape[1]
        for k in range(9):
            s_ref[k * atoms : (k + 1) * atoms, at : at + lanes] = (hot * rows[k]).astype(BF16)

    def messages(radial_at, up, at):
        lanes = up.shape[1]
        up_ref[:, at : at + lanes] = up.astype(BF16)
        for l in range(3):
            here = slice(l * channels, (l + 1) * channels)
            m_ref[here, at : at + lanes] = (
                radial_ref[here, radial_at : radial_at + lanes] * up
            ).astype(BF16)

    inverse_a, n_a = [], []
    for at in (0, cut):
        part = slice(at, at + width) if at else slice(0, cut)
        inverse, n = geometry(vx[:, part], vy[:, part], vz[:, part], part.start)
        inverse_a.append(inverse)
        n_a.append(n)
        scaled_hot(hot_one[:, part], harmonic_rows(n, weight[:, part]), part.start)
    turned_low = tuple(-x for x in n_a[0])
    scaled_hot(hot_two[:, :cut], harmonic_rows(turned_low, weight[:, :cut]), pairs)
    messages(0, nn(up_t, hot_two[:, :cut]), 0)
    messages(0, nn(up_t, hot_one[:, :cut]), pairs)
    ghost_row = lax.broadcasted_iota(jnp.int32, (plan.count * slots, width), 0)
    ghost_at = jnp.where(own_lane, -1, ghost_base + window_slot)
    hot_ghost[...] = (ghost_row == ghost_at).astype(F32).astype(BF16)
    edge_in[...] = first_rows
    info_in[...] = jnp.zeros((width, 128), BF16)
    ghost_in[...] = jnp.zeros((plan.count * slots, channels), BF16)

    for copy in first_copies:
        copy.wait()
    for d in plan.others:
        at = plan.start[d]
        ghost_in[d * slots : (d + 1) * slots, :] = recv_one[at : at + slots, :]
        tile = recv_one[at + slots : at + 2 * slots, :]
        for g in plan.members[d]:
            spot = plan.block_start[g]
            here = slice(pad + slots * g, pad + slots * (g + 1))
            edge_in[here, :] = recv_one[spot : spot + slots, :]
            info_in[here, :] = tile

    row = lax.broadcasted_iota(jnp.int32, (width, 128), 0)
    row_block = jnp.maximum(row - pad, 0) >> 4
    row_sub = plan.sub(plan.lane_offsets(row_block))
    column = lax.broadcasted_iota(jnp.int32, (width, 128), 1) >> 4
    info_own = jnp.where(column == row_sub, info_in[...].astype(F32), 0.0).astype(BF16)
    pick_row = lax.broadcasted_iota(jnp.int32, (16, 128), 0)
    pick_at = lax.broadcasted_iota(jnp.int32, (16, 128), 1) & 15
    pick = jnp.where(pick_at < 9, (pick_at * 11) >> 5, pick_at - 6) == pick_row
    incoming = nt(pick.astype(F32).astype(BF16), info_own)
    slot_in = incoming[4:5, :].astype(jnp.int32)
    slot_hot = (lax.broadcasted_iota(jnp.int32, (slots, width), 0) == slot_in).astype(F32)
    export_rows = jnp.broadcast_to(export_ref[...].astype(F32), (8, slots))
    target = nn(export_rows.astype(BF16), slot_hot.astype(BF16))[0:1, :].astype(jnp.int32)
    target = jnp.where(own_lane, second[:, cut:], target)
    weight_b = jnp.where(own_lane, live[:, cut:], incoming[3:4, :]) * norm
    back = []
    for i, v in enumerate((vx, vy, vz)):
        back.append(-jnp.where(own_lane, v[:, cut:], incoming[i : i + 1, :]))
    hot_b = (lax.broadcasted_iota(jnp.int32, (atoms, width), 0) == target).astype(F32)
    hot_back[...] = hot_b.astype(BF16)
    inverse_b, n_b = geometry(*back, pairs)
    scaled_hot(hot_b, harmonic_rows(n_b, weight_b), pairs + cut)
    ghost_up = nt(w_up_t, ghost_in[...]).astype(BF16)
    messages(cut, nn(up_t, hot_two[:, cut:]) + nn(ghost_up, hot_ghost[...]), cut)
    messages(pairs, rounded(nt(w_up_t, edge_in[...])), pairs + cut)

    amps = []
    for l, (low, high) in enumerate(DEGREE_ROWS):
        sums = nt(m_ref[l * channels : (l + 1) * channels, :], s_ref[low * atoms : high * atoms, :])
        amps += [sums[:, i * atoms : (i + 1) * atoms] for i in range(high - low)]
    power = [tables[:, l : l + 1] for l in range(3)]
    product = amps[0]
    for l, (low, high) in enumerate(DEGREE_ROWS):
        total = amps[low] * amps[low]
        for k in range(low + 1, high):
            total = total + amps[k] * amps[k]
        product = product + power[l] * total
    mixed = nn(w_mix_t, product.astype(BF16))
    species = species_ref[...]
    picker = (lax.broadcasted_iota(jnp.int32, (128, atoms), 0) == species + 3).astype(F32)
    read_rows = lax.dot_general(
        tables,
        picker,
        (((1,), (0,)), ((), ())),
        precision=lax.Precision.HIGHEST,
        preferred_element_type=F32,
    )
    base = jnp.zeros((1, atoms), F32)
    for s in range(read_ref.shape[0]):
        base = base + jnp.where(species == s, base_ref[s], 0.0)
    sigmoid = jax.nn.sigmoid(mixed)
    energy_ref[...] = jnp.sum(mixed * sigmoid * read_rows, axis=0, keepdims=True) + base
    grad_mixed = (read_rows * sigmoid * (1.0 + mixed * (1.0 - sigmoid))).astype(BF16)
    grad_product = nn(w_mix, grad_mixed)
    for l, (low, high) in enumerate(DEGREE_ROWS):
        twice = grad_product * (2.0 * power[l])
        for k in range(low, high):
            value = twice * amps[k]
            if k == 0:
                value = value + grad_product
            value = value.astype(BF16)
            g_wide[:, k * atoms : (k + 1) * atoms] = value
            g_tall[k * channels : (k + 1) * channels, :] = value

    def backward(at, radial_at, hot, n, inverse, w):
        lanes = hot.shape[1]
        here = slice(at, at + lanes)
        there = slice(radial_at, radial_at + lanes)
        source, along = 0.0, 0.0
        for l, (low, high) in enumerate(DEGREE_ROWS):
            held = nn(g_wide[:, low * atoms : high * atoms], s_ref[low * atoms : high * atoms, here])
            part = slice(l * channels, (l + 1) * channels)
            source = source + radial_ref[part, there] * held
            along = along + slope_ref[part, there] * held
        along = jnp.sum(along * up_ref[:, here].astype(F32), axis=0, keepdims=True)
        p = [None]
        for k in range(1, 9):
            l = 1 if k < 4 else 2
            gathered = nn(g_tall[k * channels : (k + 1) * channels, :], hot)
            values = m_ref[l * channels : (l + 1) * channels, here].astype(F32)
            p.append(jnp.sum(gathered * values, axis=0, keepdims=True))
        x, y, z = n
        dx = S3 * p[1] + S15 * (z * p[4] + y * p[5] - x * p[8]) - S5 * x * p[6]
        dy = S3 * p[2] + S15 * (x * p[5] + z * p[7]) + 2.0 * S5 * y * p[6]
        dz = S3 * p[3] + S15 * (x * p[4] + y * p[7] + z * p[8]) - S5 * z * p[6]
        scale = w * inverse
        radial_part = along - scale * (x * dx + y * dy + z * dz)
        g = (
            scale * dx + x * radial_part,
            scale * dy + y * radial_part,
            scale * dz + z * radial_part,
        )
        hi = [rounded(v) for v in g]
        lo = [v - h for v, h in zip(g, hi)]
        fill = jnp.zeros((10, lanes), F32)
        return source, jnp.concatenate(list(g) + [jnp.zeros((13, lanes), F32)], axis=0), (
            jnp.concatenate(hi + lo + [fill], axis=0).astype(BF16)
        )

    source_a, _, split_a = backward(
        cut, cut, hot_one[:, cut:], n_a[1], inverse_a[1], weight[:, cut:]
    )
    source_b, force_b, split_b = backward(
        pairs + cut, pairs, hot_back[...], n_b, inverse_b, weight_b
    )
    source_a = source_a.astype(BF16)
    ghost_grad = nt(hot_ghost[...], source_a)
    ghost_force = -nt(
        hot_ghost[...],
        jnp.concatenate([split_a.astype(F32), jnp.zeros((112, width), F32)], axis=0).astype(BF16),
    )
    edge_grad = jnp.transpose(source_b).astype(BF16)
    tiled = jnp.concatenate([-force_b] * 8, axis=0)
    edge_force = jnp.transpose(jnp.where(tall_group == lane_sub + 1, tiled, 0.0))
    second_copies = []
    for d in plan.others:
        at = plan.start[d]
        ghost = slice(d * slots, (d + 1) * slots)
        send_two[at : at + slots, :] = ghost_grad[ghost, :].astype(BF16)
        tile = ghost_force[ghost, :]
        for g in plan.members[d]:
            here = slice(pad + slots * g, pad + slots * (g + 1))
            tile = tile + edge_force[here, :]
            spot = plan.block_start[g]
            send_two[spot : spot + slots, :] = edge_grad[here, :]
        send_two[at + slots : at + 2 * slots, :] = tile.astype(BF16)
        part = pl.ds(at, plan.rows[d])
        copy = pltpu.make_async_remote_copy(
            src_ref=send_two.at[part],
            dst_ref=recv_two.at[part],
            send_sem=s2.at[d],
            recv_sem=r2.at[d],
            device_id=device(d, -1),
            device_id_type=MESH,
        )
        copy.start()
        second_copies.append(copy)

    source_c, _, split_c = backward(0, 0, hot_one[:, :cut], n_a[0], inverse_a[0], weight[:, :cut])
    source_d, _, split_d = backward(
        pairs, 0, hot_two[:, :cut], turned_low, inverse_a[0], weight[:, :cut]
    )
    grad_up = (
        nt(hot_two[:, cut:], source_a)
        + nt(hot_two[:, :cut], source_c.astype(BF16))
        + nt(hot_one[:, :cut], source_d.astype(BF16))
    )
    force = nt(split_a, hot_one[:, cut:]) - nt(split_a, hot_two[:, cut:])
    force = force + nt(split_b, hot_back[...])
    force = force + nt(split_c, hot_one[:, :cut]) - nt(split_c, hot_two[:, :cut])
    force = force + nt(split_d, hot_two[:, :cut]) - nt(split_d, hot_one[:, :cut])
    edge_in[...] = edge_grad
    info_in[...] = edge_force.astype(BF16)

    for copy in second_copies:
        copy.wait()
    offered_grad, offered_force = 0.0, 0.0
    for d in plan.others:
        at = plan.start[d]
        offered_grad = offered_grad + recv_two[at : at + slots, :].astype(F32)
        tile = recv_two[at + slots : at + 2 * slots, :]
        offered_force = offered_force + tile.astype(F32)
        for g in plan.members[d]:
            spot = plan.block_start[g]
            here = slice(pad + slots * g, pad + slots * (g + 1))
            edge_in[here, :] = recv_two[spot : spot + slots, :]
            info_in[here, :] = tile
    info_own = jnp.where(column == row_sub + 1, info_in[...].astype(F32), 0.0).astype(BF16)
    offered_column = lax.broadcasted_iota(jnp.int32, (slots, 128), 1)
    offered_force = jnp.where(offered_column < 16, offered_force, 0.0)
    window_hot = hot_one[:, cut:]
    grad_up = grad_up + nn(window_hot, edge_in[...]) + nn(export_hot, offered_grad.astype(BF16))
    remote_force = nn(window_hot, info_own) + nn(export_hot, offered_force.astype(BF16))
    remote_force = jnp.transpose(remote_force)
    total = force[0:3, :] + force[3:6, :]
    for j in range(8):
        total = total + remote_force[16 * j : 16 * j + 3, :] + remote_force[16 * j + 3 : 16 * j + 6, :]
    force_ref[...] = total
    grad_ref[...] = nt(grad_up.astype(BF16), w_up).astype(BF16)


def on_device(plan, *args):
    (
        node_feats,
        species,
        export_index,
        pair_first,
        pair_second,
        pair_live,
        displacement,
        w_up,
        radial_one,
        radial_two,
        radial_three,
        power_weight,
        w_mix,
        read_table,
        base_energy,
    ) = args
    atoms, channels = node_feats.shape
    pairs = pair_first.shape[0]
    slots = export_index.shape[0]
    cut = (pairs - 27 * slots) // 128 * 128
    width = pairs - cut
    ghosts = plan.count * slots
    vmem = pl.BlockSpec(memory_space=pltpu.VMEM)
    smem = pl.BlockSpec(memory_space=pltpu.SMEM)
    energy, forces, grad = pl.pallas_call(
        functools.partial(kernel, plan),
        out_shape=(
            jax.ShapeDtypeStruct((1, atoms), F32),
            jax.ShapeDtypeStruct((3, atoms), F32),
            jax.ShapeDtypeStruct((atoms, channels), BF16),
        ),
        in_specs=[vmem] * 14 + [smem],
        out_specs=(vmem,) * 3,
        scratch_shapes=[pltpu.VMEM((plan.total, channels), BF16)] * 4
        + [
            pltpu.VMEM((width, channels), BF16),
            pltpu.VMEM((width, 128), BF16),
            pltpu.VMEM((ghosts, channels), BF16),
            pltpu.VMEM((3 * channels, pairs + width), F32),
            pltpu.VMEM((3 * channels, pairs + width), F32),
            pltpu.VMEM((channels, 2 * pairs), BF16),
            pltpu.VMEM((3 * channels, 2 * pairs), BF16),
            pltpu.VMEM((9 * atoms, 2 * pairs), BF16),
            pltpu.VMEM((atoms, pairs), BF16),
            pltpu.VMEM((atoms, pairs), BF16),
            pltpu.VMEM((atoms, width), BF16),
            pltpu.VMEM((ghosts, width), BF16),
            pltpu.VMEM((channels, 9 * atoms), BF16),
            pltpu.VMEM((9 * channels, atoms), BF16),
        ]
        + [pltpu.SemaphoreType.DMA((plan.count,))] * 4,
        compiler_params=pltpu.CompilerParams(
            collective_id=0, has_side_effects=True, vmem_limit_bytes=48 * 1024 * 1024
        ),
    )(
        node_feats,
        species.reshape(1, atoms),
        export_index.reshape(1, slots),
        pair_first.reshape(1, pairs),
        pair_second.reshape(1, pairs),
        pair_live.reshape(1, pairs),
        displacement,
        w_up,
        radial_one,
        radial_two,
        radial_three,
        power_weight,
        w_mix,
        read_table,
        base_energy,
    )
    return energy.reshape(atoms), forces, grad


def solution(mesh):
    every = ("groups", "gx", "gy", "gz")
    plan = Plan(tuple(mesh.shape[a] for a in ("gx", "gy", "gz")), 16)
    in_specs = (
        (P(every, None),) + (P(every),) * 5 + (P(None, every),) + (P(),) * 8
    )
    out_specs = (P(every), P(None, every), P(every, None))
    return jax.shard_map(
        functools.partial(on_device, plan),
        mesh=mesh,
        in_specs=in_specs,
        out_specs=out_specs,
        check_vma=False,
    )
```

```python
import functools
import math

import jax
import jax.numpy as jnp
from jax import lax
from jax.experimental import pallas as pl
from jax.experimental.pallas import tpu as pltpu
from jax.sharding import PartitionSpec as P

CUTOFF = 5.0
S3 = math.sqrt(3.0)
S5 = math.sqrt(5.0)
S15 = math.sqrt(15.0)
F32 = jnp.float32
BF16 = jnp.bfloat16
MESH = pl.DeviceIdType.MESH
DEGREE_ROWS = ((0, 1), (1, 4), (4, 9))


def nn(a, b):
    return lax.dot_general(a, b, (((1,), (0,)), ((), ())), preferred_element_type=F32)


def nt(a, b):
    return lax.dot_general(a, b, (((1,), (1,)), ((), ())), preferred_element_type=F32)


def rounded(x):
    return x.astype(BF16).astype(F32)


def split_weights(w):
    depth, width = w.shape
    hi = rounded(w)
    stack = jnp.concatenate([hi, hi, w - hi], axis=0)
    rows = -(-3 * depth // 128) * 128
    stack = jnp.concatenate([stack, jnp.zeros((rows - 3 * depth, width), F32)], axis=0)
    columns = -(-width // 128) * 128
    if columns > width:
        stack = jnp.concatenate([stack, jnp.zeros((rows, columns - width), F32)], axis=1)
    return jnp.transpose(stack)[:width].astype(BF16)


def split_values(h, rows):
    hi = rounded(h)
    parts = [hi, h - hi, hi]
    spare = rows - 3 * h.shape[0]
    if spare:
        parts.append(jnp.zeros((spare, h.shape[1]), F32))
    return jnp.concatenate(parts, axis=0).astype(BF16)


def flipped(w):
    return jnp.transpose(w.astype(F32)).astype(BF16)


def polynomial(x, coefficients):
    total = coefficients[-1]
    for c in coefficients[-2::-1]:
        total = total * x + c
    return total


SIN_SERIES = [(-1.0) ** i / math.factorial(2 * i + 1) for i in range(7)]
COS_SERIES = [(-1.0) ** i / math.factorial(2 * i) for i in range(8)]


def direction(vx, vy, vz):
    square = vx * vx + vy * vy + vz * vz
    inverse = lax.rsqrt(square)
    return square * inverse, inverse, (vx * inverse, vy * inverse, vz * inverse)


def radial_network(distance, inverse, orders, one, two, three):
    lanes = distance.shape[1]
    x = distance * (1.0 / CUTOFF)
    phase = math.pi * x - 0.5 * math.pi
    square = phase * phase
    sine = polynomial(square, COS_SERIES)
    cosine = -phase * polynomial(square, SIN_SERIES)
    sines, cosines = [sine], [cosine]
    for _ in range(orders - 1):
        s, c = sines[-1], cosines[-1]
        sines.append(s * cosine + c * sine)
        cosines.append(c * cosine - s * sine)
    x2 = x * x
    x5 = x2 * x2 * x
    envelope = 1.0 - x5 * x * (28.0 - 48.0 * x + 21.0 * x2)
    slope = -168.0 * x5 * (1.0 - x) * (1.0 - x)
    scale = math.sqrt(2.0 / CUTOFF) * inverse
    factor = scale * envelope
    factor_slope = scale * (slope * (1.0 / CUTOFF) - envelope * inverse)
    sin_rows = jnp.concatenate(sines, axis=0)
    cos_rows = jnp.concatenate(cosines, axis=0)
    number = lax.broadcasted_iota(jnp.int32, (orders, lanes), 0).astype(F32) + 1.0
    basis = sin_rows * factor
    basis_slope = cos_rows * (number * (math.pi / CUTOFF)) * factor + sin_rows * factor_slope
    both = jnp.concatenate([basis, basis_slope], axis=1)
    for weights in (one, two):
        both = nn(weights, split_values(both, weights.shape[1]))
        value, tangent = both[:, :lanes], both[:, lanes:]
        sigmoid = jax.nn.sigmoid(value)
        hidden = value * sigmoid
        tangent = tangent * (sigmoid + hidden * (1.0 - sigmoid))
        both = jnp.concatenate([hidden, tangent], axis=1)
    both = nn(three, split_values(both, three.shape[1]))
    return both[:, :lanes], both[:, lanes:]


def harmonic_rows(n, w):
    x, y, z = n
    wx, wy, wz = (w * x, w * y, w * z)
    return (
        w,
        S3 * wx,
        S3 * wy,
        S3 * wz,
        S15 * wx * z,
        S15 * wx * y,
        S5 * (wy * y - 0.5 * (wx * x + wz * z)),
        S15 * wy * z,
        0.5 * S15 * (wz * z - wx * x),
    )


class Plan:
    def __init__(self, sizes, slots):
        self.sizes = sizes
        self.slots = slots
        self.classes = tuple(2 if n == 2 else 3 for n in sizes)
        self.subs = tuple(2 if n == 2 else 1 for n in sizes)
        self.count = math.prod(self.classes)
        self.members = [[] for _ in range(self.count)]
        self.sub_of = {}
        for g in range(27):
            o = (g // 9, g // 3 % 3, g % 3)
            index, sub = self.index(o), self.sub(o)
            self.members[index].append(g)
            self.sub_of[g] = sub
        self.own = self.index((1, 1, 1))
        self.others = sorted(
            (d for d in range(self.count) if d != self.own), key=lambda d: self.shift(d)[0] == 0
        )
        self.start, self.rows, self.block_start = {}, {}, {}
        total = 0
        for d in self.others:
            self.start[d] = total
            self.rows[d] = slots * (2 + len(self.members[d]))
            for i, g in enumerate(self.members[d]):
                self.block_start[g] = total + slots * (2 + i)
            total += self.rows[d]
        self.total = total

    def index(self, o, turned=False):
        value = 0
        for part, n, classes in zip(o, self.sizes, self.classes):
            part = part & 1 if n == 2 else (2 - part if turned else part)
            value = value * classes + part
        return value

    def sub(self, o):
        value = 0
        for part, n, subs in zip(o, self.sizes, self.subs):
            value = value * subs + (part >> 1 if n == 2 else part * 0)
        return value

    def class_of_block(self, g):
        return self.index((g // 9, g // 3 % 3, g % 3))

    def shift(self, d):
        out = []
        for classes in reversed(self.classes):
            out.append(d % classes - 1)
            d //= classes
        return tuple(reversed(out))

    def lane_offsets(self, g):
        a = (g * 57) >> 9
        rest = g - 9 * a
        b = (rest * 11) >> 5
        return (a, b, rest - 3 * b)


def kernel(
    plan,
    feats_far,
    species_far,
    export_far,
    first_far,
    second_far,
    live_far,
    disp_far,
    w_up_far,
    one_far,
    two_far,
    three_far,
    power_far,
    w_mix_far,
    read_far,
    base_ref,
    energy_ref,
    force_ref,
    grad_ref,
    send_one,
    recv_one,
    send_two,
    recv_two,
    edge_in,
    info_in,
    ghost_in,
    radial_ref,
    slope_ref,
    up_ref,
    m_ref,
    s_ref,
    hot_one,
    hot_two,
    hot_back,
    hot_ghost,
    g_wide,
    g_tall,
    s1,
    r1,
    s2,
    r2,
    load_sem,
    feats_ref,
    species_ref,
    export_ref,
    first_ref,
    second_ref,
    live_ref,
    disp_ref,
    w_up_ref,
    one_ref,
    two_ref,
    three_ref,
    power_ref,
    w_mix_ref,
    read_ref,
):
    atoms, channels = feats_ref.shape
    pairs = first_ref.shape[1]
    slots = plan.slots
    head = pairs - 27 * slots
    cut = head // 128 * 128
    width = pairs - cut
    pad = head - cut
    orders = one_ref.shape[0]
    norm = 1.0 / math.sqrt(2.0 * pairs / atoms)

    me = tuple(lax.axis_index(a) for a in ("groups", "gx", "gy", "gz"))

    def device(d, turn):
        place = [me[0]]
        for here, step, n in zip(me[1:], plan.shift(d), plan.sizes):
            place.append(lax.rem(here + turn * step + n, n))
        return tuple(place)

    barrier = pltpu.get_barrier_semaphore()
    for d in plan.others:
        pl.semaphore_signal(barrier, inc=1, device_id=device(d, 1), device_id_type=MESH)

    order = (
        (first_far, first_ref),
        (second_far, second_ref),
        (feats_far, feats_ref),
        (disp_far, disp_ref),
        (live_far, live_ref),
        (export_far, export_ref),
        (one_far, one_ref),
        (two_far, two_ref),
        (three_far, three_ref),
        (w_up_far, w_up_ref),
        (w_mix_far, w_mix_ref),
        (species_far, species_ref),
        (power_far, power_ref),
        (read_far, read_ref),
    )
    loads = [
        pltpu.make_async_copy(far, near, load_sem.at[i]) for i, (far, near) in enumerate(order)
    ]
    for load in loads:
        load.start()

    lane = lax.broadcasted_iota(jnp.int32, (1, width), 1)
    block = jnp.maximum(lane - pad, 0) >> 4
    offsets = plan.lane_offsets(block)
    own_lane = jnp.logical_or(lane < pad, block == 13)
    lane_sub = plan.sub(offsets)
    ghost_base = plan.index(offsets, turned=True) * slots

    for load in loads[:6]:
        load.wait()
    first = first_ref[...]
    second = second_ref[...]
    live = live_ref[...].astype(F32)
    vx, vy, vz = disp_ref[0:1, :], disp_ref[1:2, :], disp_ref[2:3, :]

    atom_row = lax.broadcasted_iota(jnp.int32, (atoms, pairs), 0)
    hot_one[...] = (atom_row == first).astype(F32).astype(BF16)
    hot_two[...] = (atom_row == second).astype(F32).astype(BF16)
    export_hot = (
        (lax.broadcasted_iota(jnp.int32, (atoms, slots), 0) == export_ref[...])
        .astype(F32)
        .astype(BF16)
    )
    feats = feats_ref[...]

    window_slot = (second[:, cut:] - atoms) & (slots - 1)
    rows16 = []
    for v in (vx, vy, vz):
        piece = v[:, cut:]
        for _ in range(3):
            hi = rounded(piece)
            rows16.append(hi)
            piece = piece - hi
    rows16.append(live[:, cut:])
    rows16.append(window_slot.astype(F32))
    rows16.append(jnp.zeros((16 - len(rows16), width), F32))
    group16 = jnp.concatenate(rows16, axis=0)
    tall_group = lax.broadcasted_iota(jnp.int32, (128, width), 0) >> 4
    tiled = jnp.concatenate([group16] * 8, axis=0)
    info_rows = jnp.transpose(jnp.where(tall_group == lane_sub, tiled, 0.0))

    def transposed_dot(a, b):
        return nn(jnp.transpose(a.astype(F32)).astype(BF16), b)

    first_rows = transposed_dot(hot_one[:, cut:], feats).astype(BF16)
    offered = transposed_dot(
        jnp.concatenate([export_hot.astype(F32), jnp.zeros((atoms, 128 - slots), F32)], axis=1),
        feats,
    )[:slots].astype(BF16)
    for d in plan.others:
        at = plan.start[d]
        send_one[at : at + slots, :] = offered
        tile = None
        for g in plan.members[d]:
            part = info_rows[pad + slots * g : pad + slots * (g + 1), :]
            tile = part if tile is None else tile + part
            spot = plan.block_start[g]
            send_one[spot : spot + slots, :] = first_rows[pad + slots * g : pad + slots * (g + 1), :]
        send_one[at + slots : at + 2 * slots, :] = tile.astype(BF16)

    pl.semaphore_wait(barrier, len(plan.others))
    first_copies = []
    for d in plan.others:
        part = pl.ds(plan.start[d], plan.rows[d])
        copy = pltpu.make_async_remote_copy(
            src_ref=send_one.at[part],
            dst_ref=recv_one.at[part],
            send_sem=s1.at[d],
            recv_sem=r1.at[d],
            device_id=device(d, 1),
            device_id_type=MESH,
        )
        copy.start()
        first_copies.append(copy)

    for load in loads[6:]:
        load.wait()
    one = split_weights(one_ref[...])
    two = split_weights(two_ref[...])
    three = split_weights(three_ref[...])
    w_up = w_up_ref[...]
    w_up_t = flipped(w_up)
    w_mix = w_mix_ref[...]
    w_mix_t = flipped(w_mix)
    tables = jnp.transpose(
        jnp.concatenate(
            [
                power_ref[...],
                read_ref[...],
                jnp.zeros((128 - 3 - read_ref.shape[0], channels), F32),
            ],
            axis=0,
        )
    )
    up_t = nt(w_up_t, feats).astype(BF16)

    weight = live * norm
    edges = []

    def geometry(ax, ay, az, at):
        distance, inverse, n = direction(ax, ay, az)
        radial, slope = radial_network(distance, inverse, orders, one, two, three)
        lanes = ax.shape[1]
        radial_ref[:, at : at + lanes] = radial
        slope_ref[:, at : at + lanes] = slope
        return inverse, n

    def scaled_hot(hot, rows, at):
        lanes = hot.shape[1]
        for k in range(9):
            scale = jnp.broadcast_to(rows[k], (16, lanes)).astype(BF16)
            scale = jnp.concatenate([scale] * (atoms // 16), axis=0)
            s_ref[k * atoms : (k + 1) * atoms, at : at + lanes] = hot * scale

    def messages(radial_at, up, at):
        lanes = up.shape[1]
        up_ref[:, at : at + lanes] = up.astype(BF16)
        for l in range(3):
            here = slice(l * channels, (l + 1) * channels)
            m_ref[here, at : at + lanes] = (
                radial_ref[here, radial_at : radial_at + lanes] * up
            ).astype(BF16)

    inverse_a, n_a = [], []
    for at in (0, cut):
        part = slice(at, at + width) if at else slice(0, cut)
        inverse, n = geometry(vx[:, part], vy[:, part], vz[:, part], part.start)
        inverse_a.append(inverse)
        n_a.append(n)
        scaled_hot(hot_one[:, part], harmonic_rows(n, weight[:, part]), part.start)
    turned_low = tuple(-x for x in n_a[0])
    scaled_hot(hot_two[:, :cut], harmonic_rows(turned_low, weight[:, :cut]), pairs)
    messages(0, nn(up_t, hot_two[:, :cut]), 0)
    messages(0, nn(up_t, hot_one[:, :cut]), pairs)
    ghost_row = lax.broadcasted_iota(jnp.int32, (plan.count * slots, width), 0)
    ghost_at = jnp.where(own_lane, -1, ghost_base + window_slot)
    hot_ghost[...] = (ghost_row == ghost_at).astype(F32).astype(BF16)
    edge_in[...] = first_rows
    info_in[...] = jnp.zeros((width, 128), BF16)
    ghost_in[...] = jnp.zeros((plan.count * slots, channels), BF16)

    row = lax.broadcasted_iota(jnp.int32, (width, 128), 0)
    row_block = jnp.maximum(row - pad, 0) >> 4
    row_sub = plan.sub(plan.lane_offsets(row_block))
    column = lax.broadcasted_iota(jnp.int32, (width, 128), 1) >> 4
    mask_one = (column == row_sub).astype(F32).astype(BF16)
    mask_two = (column == row_sub + 1).astype(F32).astype(BF16)
    pick_row = lax.broadcasted_iota(jnp.int32, (16, 128), 0)
    pick_at = lax.broadcasted_iota(jnp.int32, (16, 128), 1) & 15
    pick = jnp.where(pick_at < 9, (pick_at * 11) >> 5, pick_at - 6) == pick_row
    pick = pick.astype(F32).astype(BF16)
    power = [tables[:, l : l + 1] for l in range(3)]
    species = species_ref[...]
    picker = (lax.broadcasted_iota(jnp.int32, (128, atoms), 0) == species + 3).astype(F32)
    read_rows = lax.dot_general(
        tables,
        picker,
        (((1,), (0,)), ((), ())),
        precision=lax.Precision.HIGHEST,
        preferred_element_type=F32,
    )
    base = jnp.zeros((1, atoms), F32)
    for s in range(read_ref.shape[0]):
        base = base + jnp.where(species == s, base_ref[s], 0.0)

    def amps_of(degree, start, stop):
        low, high = DEGREE_ROWS[degree]
        return nt(
            m_ref[degree * channels : (degree + 1) * channels, start:stop],
            s_ref[low * atoms : high * atoms, start:stop],
        )

    early = [amps_of(l, 0, cut) + amps_of(l, pairs, pairs + cut) for l in range(3)]

    for copy in first_copies:
        copy.wait_recv()
    for d in plan.others:
        at = plan.start[d]
        ghost_in[d * slots : (d + 1) * slots, :] = recv_one[at : at + slots, :]
        tile = recv_one[at + slots : at + 2 * slots, :]
        for g in plan.members[d]:
            spot = plan.block_start[g]
            here = slice(pad + slots * g, pad + slots * (g + 1))
            edge_in[here, :] = recv_one[spot : spot + slots, :]
            info_in[here, :] = tile

    info_own = info_in[...] * mask_one
    incoming = nt(pick, info_own)
    slot_in = incoming[4:5, :].astype(jnp.int32)
    slot_hot = (lax.broadcasted_iota(jnp.int32, (slots, width), 0) == slot_in).astype(F32)
    export_rows = jnp.broadcast_to(export_ref[...].astype(F32), (8, slots))
    target = nn(export_rows.astype(BF16), slot_hot.astype(BF16))[0:1, :].astype(jnp.int32)
    target = jnp.where(own_lane, second[:, cut:], target)
    weight_b = jnp.where(own_lane, live[:, cut:], incoming[3:4, :]) * norm
    back = []
    for i, v in enumerate((vx, vy, vz)):
        back.append(-jnp.where(own_lane, v[:, cut:], incoming[i : i + 1, :]))
    hot_b = (lax.broadcasted_iota(jnp.int32, (atoms, width), 0) == target).astype(F32)
    hot_b = hot_b.astype(BF16)
    hot_back[...] = hot_b
    inverse_b, n_b = geometry(*back, pairs)
    scaled_hot(hot_b, harmonic_rows(n_b, weight_b), pairs + cut)
    ghost_up = nt(w_up_t, ghost_in[...]).astype(BF16)
    messages(cut, nn(up_t, hot_two[:, cut:]) + nn(ghost_up, hot_ghost[...]), cut)
    messages(pairs, rounded(nt(w_up_t, edge_in[...])), pairs + cut)

    amps = []
    for l, (low, high) in enumerate(DEGREE_ROWS):
        sums = early[l] + amps_of(l, cut, pairs) + amps_of(l, pairs + cut, 2 * pairs)
        amps += [sums[:, i * atoms : (i + 1) * atoms] for i in range(high - low)]
    product = amps[0]
    for l, (low, high) in enumerate(DEGREE_ROWS):
        total = amps[low] * amps[low]
        for k in range(low + 1, high):
            total = total + amps[k] * amps[k]
        product = product + power[l] * total
    mixed = nn(w_mix_t, product.astype(BF16))
    sigmoid = jax.nn.sigmoid(mixed)
    energy_ref[...] = jnp.sum(mixed * sigmoid * read_rows, axis=0, keepdims=True) + base
    grad_mixed = (read_rows * sigmoid * (1.0 + mixed * (1.0 - sigmoid))).astype(BF16)
    grad_product = nn(w_mix, grad_mixed)
    for l, (low, high) in enumerate(DEGREE_ROWS):
        twice = grad_product * (2.0 * power[l])
        for k in range(low, high):
            value = twice * amps[k]
            if k == 0:
                value = value + grad_product
            value = value.astype(BF16)
            g_wide[:, k * atoms : (k + 1) * atoms] = value
            g_tall[k * channels : (k + 1) * channels, :] = value

    def backward(at, radial_at, hot, n, inverse, w):
        lanes = hot.shape[1]
        here = slice(at, at + lanes)
        there = slice(radial_at, radial_at + lanes)
        source, along = 0.0, 0.0
        for l, (low, high) in enumerate(DEGREE_ROWS):
            held = nn(g_wide[:, low * atoms : high * atoms], s_ref[low * atoms : high * atoms, here])
            part = slice(l * channels, (l + 1) * channels)
            source = source + radial_ref[part, there] * held
            along = along + slope_ref[part, there] * held
        along = jnp.sum(along * up_ref[:, here].astype(F32), axis=0, keepdims=True)
        p = [None]
        for k in range(1, 9):
            l = 1 if k < 4 else 2
            gathered = nn(g_tall[k * channels : (k + 1) * channels, :], hot)
            values = m_ref[l * channels : (l + 1) * channels, here].astype(F32)
            p.append(jnp.sum(gathered * values, axis=0, keepdims=True))
        x, y, z = n
        dx = S3 * p[1] + S15 * (z * p[4] + y * p[5] - x * p[8]) - S5 * x * p[6]
        dy = S3 * p[2] + S15 * (x * p[5] + z * p[7]) + 2.0 * S5 * y * p[6]
        dz = S3 * p[3] + S15 * (x * p[4] + y * p[7] + z * p[8]) - S5 * z * p[6]
        scale = w * inverse
        radial_part = along - scale * (x * dx + y * dy + z * dz)
        g = (
            scale * dx + x * radial_part,
            scale * dy + y * radial_part,
            scale * dz + z * radial_part,
        )
        hi = [rounded(v) for v in g]
        lo = [v - h for v, h in zip(g, hi)]
        fill = jnp.zeros((10, lanes), F32)
        return source, jnp.concatenate(list(g) + [jnp.zeros((13, lanes), F32)], axis=0), (
            jnp.concatenate(hi + lo + [fill], axis=0).astype(BF16)
        )

    source_a, _, split_a = backward(
        cut, cut, hot_one[:, cut:], n_a[1], inverse_a[1], weight[:, cut:]
    )
    source_b, force_b, split_b = backward(
        pairs + cut, pairs, hot_back[...], n_b, inverse_b, weight_b
    )
    source_a = source_a.astype(BF16)
    ghost_grad = nt(hot_ghost[...], source_a)
    ghost_force = -nt(
        hot_ghost[...],
        jnp.concatenate([split_a.astype(F32), jnp.zeros((112, width), F32)], axis=0).astype(BF16),
    )
    edge_grad = jnp.transpose(source_b).astype(BF16)
    tiled = jnp.concatenate([-force_b] * 8, axis=0)
    edge_force = jnp.transpose(jnp.where(tall_group == lane_sub + 1, tiled, 0.0))
    second_copies = []
    for d in plan.others:
        at = plan.start[d]
        ghost = slice(d * slots, (d + 1) * slots)
        send_two[at : at + slots, :] = ghost_grad[ghost, :].astype(BF16)
        tile = ghost_force[ghost, :]
        for g in plan.members[d]:
            here = slice(pad + slots * g, pad + slots * (g + 1))
            tile = tile + edge_force[here, :]
            spot = plan.block_start[g]
            send_two[spot : spot + slots, :] = edge_grad[here, :]
        send_two[at + slots : at + 2 * slots, :] = tile.astype(BF16)
        part = pl.ds(at, plan.rows[d])
        copy = pltpu.make_async_remote_copy(
            src_ref=send_two.at[part],
            dst_ref=recv_two.at[part],
            send_sem=s2.at[d],
            recv_sem=r2.at[d],
            device_id=device(d, -1),
            device_id_type=MESH,
        )
        copy.start()
        second_copies.append(copy)

    source_c, _, split_c = backward(0, 0, hot_one[:, :cut], n_a[0], inverse_a[0], weight[:, :cut])
    source_d, _, split_d = backward(
        pairs, 0, hot_two[:, :cut], turned_low, inverse_a[0], weight[:, :cut]
    )
    grad_up = (
        nt(hot_two[:, cut:], source_a)
        + nt(hot_two[:, :cut], source_c.astype(BF16))
        + nt(hot_one[:, :cut], source_d.astype(BF16))
    )
    force = nt(split_a, hot_one[:, cut:]) - nt(split_a, hot_two[:, cut:])
    force = force + nt(split_b, hot_back[...])
    force = force + nt(split_c, hot_one[:, :cut]) - nt(split_c, hot_two[:, :cut])
    force = force + nt(split_d, hot_two[:, :cut]) - nt(split_d, hot_one[:, :cut])
    edge_in[...] = edge_grad
    info_in[...] = edge_force.astype(BF16)

    for copy in second_copies:
        copy.wait_recv()
    offered_grad, offered_force = 0.0, 0.0
    for d in plan.others:
        at = plan.start[d]
        offered_grad = offered_grad + recv_two[at : at + slots, :].astype(F32)
        tile = recv_two[at + slots : at + 2 * slots, :]
        offered_force = offered_force + tile.astype(F32)
        for g in plan.members[d]:
            spot = plan.block_start[g]
            here = slice(pad + slots * g, pad + slots * (g + 1))
            edge_in[here, :] = recv_two[spot : spot + slots, :]
            info_in[here, :] = tile
    info_own = info_in[...] * mask_two
    offered_column = lax.broadcasted_iota(jnp.int32, (slots, 128), 1)
    offered_force = jnp.where(offered_column < 16, offered_force, 0.0)
    window_hot = hot_one[:, cut:]
    grad_up = grad_up + nn(window_hot, edge_in[...]) + nn(export_hot, offered_grad.astype(BF16))
    remote_force = nn(window_hot, info_own) + nn(export_hot, offered_force.astype(BF16))
    remote_force = jnp.transpose(remote_force)
    total = force[0:3, :] + force[3:6, :]
    for j in range(8):
        total = total + remote_force[16 * j : 16 * j + 3, :] + remote_force[16 * j + 3 : 16 * j + 6, :]
    for copy in first_copies + second_copies:
        copy.wait_send()
    force_ref[...] = total
    grad_ref[...] = nt(grad_up.astype(BF16), w_up).astype(BF16)


def place(a_ref, b_ref, c_ref, a_out, b_out, c_out, sem):
    pairs = ((a_ref, a_out), (b_ref, b_out), (c_ref, c_out))
    copies = [pltpu.make_async_copy(a, b, sem.at[i]) for i, (a, b) in enumerate(pairs)]
    for copy in copies:
        copy.start()
    for copy in copies:
        copy.wait()


def on_device(plan, *args):
    (
        node_feats,
        species,
        export_index,
        pair_first,
        pair_second,
        pair_live,
        displacement,
        w_up,
        radial_one,
        radial_two,
        radial_three,
        power_weight,
        w_mix,
        read_table,
        base_energy,
    ) = args
    atoms, channels = node_feats.shape
    pairs = pair_first.shape[0]
    slots = export_index.shape[0]
    cut = (pairs - 27 * slots) // 128 * 128
    width = pairs - cut
    ghosts = plan.count * slots
    vmem = pl.BlockSpec(memory_space=pltpu.VMEM)
    smem = pl.BlockSpec(memory_space=pltpu.SMEM)
    operands = (
        node_feats,
        species.reshape(1, atoms),
        export_index.reshape(1, slots),
        pair_first.reshape(1, pairs),
        pair_second.reshape(1, pairs),
        pair_live.reshape(1, pairs),
        displacement,
        w_up,
        radial_one,
        radial_two,
        radial_three,
        power_weight,
        w_mix,
        read_table,
    )
    energy, forces, grad = pl.pallas_call(
        functools.partial(kernel, plan),
        out_shape=(
            jax.ShapeDtypeStruct((1, atoms), F32),
            jax.ShapeDtypeStruct((3, atoms), F32),
            jax.ShapeDtypeStruct((atoms, channels), BF16),
        ),
        in_specs=[pl.BlockSpec(memory_space=pltpu.HBM)] * 14 + [smem],
        out_specs=(vmem,) * 3,
        scratch_shapes=[pltpu.VMEM((plan.total, channels), BF16)] * 4
        + [
            pltpu.VMEM((width, channels), BF16),
            pltpu.VMEM((width, 128), BF16),
            pltpu.VMEM((ghosts, channels), BF16),
            pltpu.VMEM((3 * channels, pairs + width), F32),
            pltpu.VMEM((3 * channels, pairs + width), F32),
            pltpu.VMEM((channels, 2 * pairs), BF16),
            pltpu.VMEM((3 * channels, 2 * pairs), BF16),
            pltpu.VMEM((9 * atoms, 2 * pairs), BF16),
            pltpu.VMEM((atoms, pairs), BF16),
            pltpu.VMEM((atoms, pairs), BF16),
            pltpu.VMEM((atoms, width), BF16),
            pltpu.VMEM((ghosts, width), BF16),
            pltpu.VMEM((channels, 9 * atoms), BF16),
            pltpu.VMEM((9 * channels, atoms), BF16),
        ]
        + [pltpu.SemaphoreType.DMA((plan.count,))] * 4
        + [pltpu.SemaphoreType.DMA((len(operands),))]
        + [pltpu.VMEM(v.shape, v.dtype) for v in operands],
        compiler_params=pltpu.CompilerParams(
            collective_id=0, has_side_effects=True, vmem_limit_bytes=64 * 1024 * 1024
        ),
    )(*operands, base_energy)
    results = (energy, forces, grad)
    energy, forces, grad = pl.pallas_call(
        place,
        out_shape=tuple(jax.ShapeDtypeStruct(v.shape, v.dtype) for v in results),
        in_specs=[vmem] * 3,
        out_specs=(pl.BlockSpec(memory_space=pl.ANY),) * 3,
        scratch_shapes=[pltpu.SemaphoreType.DMA((3,))],
        compiler_params=pltpu.CompilerParams(has_side_effects=True),
    )(*results)
    return energy.reshape(atoms), forces, grad


def solution(mesh):
    every = ("groups", "gx", "gy", "gz")
    plan = Plan(tuple(mesh.shape[a] for a in ("gx", "gy", "gz")), 16)
    in_specs = (
        (P(every, None),) + (P(every),) * 5 + (P(None, every),) + (P(),) * 8
    )
    out_specs = (P(every), P(None, every), P(every, None))
    return jax.shard_map(
        functools.partial(on_device, plan),
        mesh=mesh,
        in_specs=in_specs,
        out_specs=out_specs,
        check_vma=False,
    )
```

```python
import functools
import math

import jax
import jax.numpy as jnp
from jax import lax
from jax.experimental import pallas as pl
from jax.experimental.pallas import tpu as pltpu
from jax.sharding import PartitionSpec as P

CUTOFF = 5.0
S3 = math.sqrt(3.0)
S5 = math.sqrt(5.0)
S15 = math.sqrt(15.0)
F32 = jnp.float32
BF16 = jnp.bfloat16
MESH = pl.DeviceIdType.MESH
DEGREE_ROWS = ((0, 1), (1, 4), (4, 9))


def nn(a, b):
    return lax.dot_general(a, b, (((1,), (0,)), ((), ())), preferred_element_type=F32)


def nt(a, b):
    return lax.dot_general(a, b, (((1,), (1,)), ((), ())), preferred_element_type=F32)


def rounded(x):
    return x.astype(BF16).astype(F32)


def split_weights(w):
    depth, width = w.shape
    hi = rounded(w)
    stack = jnp.concatenate([hi, hi, w - hi], axis=0)
    rows = -(-3 * depth // 128) * 128
    stack = jnp.concatenate([stack, jnp.zeros((rows - 3 * depth, width), F32)], axis=0)
    columns = -(-width // 128) * 128
    if columns > width:
        stack = jnp.concatenate([stack, jnp.zeros((rows, columns - width), F32)], axis=1)
    return jnp.transpose(stack)[:width].astype(BF16)


def split_values(h, rows):
    hi = rounded(h)
    parts = [hi, h - hi, hi]
    spare = rows - 3 * h.shape[0]
    if spare:
        parts.append(jnp.zeros((spare, h.shape[1]), F32))
    return jnp.concatenate(parts, axis=0).astype(BF16)


def flipped(w):
    return jnp.transpose(w.astype(F32)).astype(BF16)


def polynomial(x, coefficients):
    total = coefficients[-1]
    for c in coefficients[-2::-1]:
        total = total * x + c
    return total


SIN_SERIES = [(-1.0) ** i / math.factorial(2 * i + 1) for i in range(7)]
COS_SERIES = [(-1.0) ** i / math.factorial(2 * i) for i in range(8)]


def direction(vx, vy, vz):
    square = vx * vx + vy * vy + vz * vz
    inverse = lax.rsqrt(square)
    return square * inverse, inverse, (vx * inverse, vy * inverse, vz * inverse)


def radial_network(distance, inverse, orders, one, two, three):
    lanes = distance.shape[1]
    x = distance * (1.0 / CUTOFF)
    phase = math.pi * x - 0.5 * math.pi
    square = phase * phase
    sine = polynomial(square, COS_SERIES)
    cosine = -phase * polynomial(square, SIN_SERIES)
    sines, cosines = [sine], [cosine]
    for _ in range(orders - 1):
        s, c = sines[-1], cosines[-1]
        sines.append(s * cosine + c * sine)
        cosines.append(c * cosine - s * sine)
    x2 = x * x
    x5 = x2 * x2 * x
    envelope = 1.0 - x5 * x * (28.0 - 48.0 * x + 21.0 * x2)
    slope = -168.0 * x5 * (1.0 - x) * (1.0 - x)
    scale = math.sqrt(2.0 / CUTOFF) * inverse
    factor = scale * envelope
    factor_slope = scale * (slope * (1.0 / CUTOFF) - envelope * inverse)
    sin_rows = jnp.concatenate(sines, axis=0)
    cos_rows = jnp.concatenate(cosines, axis=0)
    number = lax.broadcasted_iota(jnp.int32, (orders, lanes), 0).astype(F32) + 1.0
    basis = sin_rows * factor
    basis_slope = cos_rows * (number * (math.pi / CUTOFF)) * factor + sin_rows * factor_slope
    both = jnp.concatenate([basis, basis_slope], axis=1)
    for weights in (one, two):
        both = nn(weights, split_values(both, weights.shape[1]))
        value, tangent = both[:, :lanes], both[:, lanes:]
        sigmoid = jax.nn.sigmoid(value)
        hidden = value * sigmoid
        tangent = tangent * (sigmoid + hidden * (1.0 - sigmoid))
        both = jnp.concatenate([hidden, tangent], axis=1)
    both = nn(three, split_values(both, three.shape[1]))
    return both[:, :lanes], both[:, lanes:]


def harmonic_rows(n, w):
    x, y, z = n
    wx, wy, wz = (w * x, w * y, w * z)
    return (
        w,
        S3 * wx,
        S3 * wy,
        S3 * wz,
        S15 * wx * z,
        S15 * wx * y,
        S5 * (wy * y - 0.5 * (wx * x + wz * z)),
        S15 * wy * z,
        0.5 * S15 * (wz * z - wx * x),
    )


class Plan:
    def __init__(self, sizes, slots):
        self.sizes = sizes
        self.slots = slots
        self.classes = tuple(2 if n == 2 else 3 for n in sizes)
        self.subs = tuple(2 if n == 2 else 1 for n in sizes)
        self.count = math.prod(self.classes)
        self.members = [[] for _ in range(self.count)]
        self.sub_of = {}
        for g in range(27):
            o = (g // 9, g // 3 % 3, g % 3)
            index, sub = self.index(o), self.sub(o)
            self.members[index].append(g)
            self.sub_of[g] = sub
        self.own = self.index((1, 1, 1))
        self.others = sorted(
            (d for d in range(self.count) if d != self.own), key=lambda d: self.shift(d)[0] == 0
        )
        self.start, self.rows, self.block_start = {}, {}, {}
        total = 0
        for d in self.others:
            self.start[d] = total
            self.rows[d] = slots * (2 + len(self.members[d]))
            for i, g in enumerate(self.members[d]):
                self.block_start[g] = total + slots * (2 + i)
            total += self.rows[d]
        self.total = total

    def index(self, o, turned=False):
        value = 0
        for part, n, classes in zip(o, self.sizes, self.classes):
            part = part & 1 if n == 2 else (2 - part if turned else part)
            value = value * classes + part
        return value

    def sub(self, o):
        value = 0
        for part, n, subs in zip(o, self.sizes, self.subs):
            value = value * subs + (part >> 1 if n == 2 else part * 0)
        return value

    def class_of_block(self, g):
        return self.index((g // 9, g // 3 % 3, g % 3))

    def shift(self, d):
        out = []
        for classes in reversed(self.classes):
            out.append(d % classes - 1)
            d //= classes
        return tuple(reversed(out))

    def lane_offsets(self, g):
        a = (g * 57) >> 9
        rest = g - 9 * a
        b = (rest * 11) >> 5
        return (a, b, rest - 3 * b)


def kernel(
    plan,
    feats_far,
    species_far,
    export_far,
    first_far,
    second_far,
    live_far,
    disp_far,
    w_up_far,
    one_far,
    two_far,
    three_far,
    power_far,
    w_mix_far,
    read_far,
    base_far,
    energy_ref,
    force_ref,
    grad_ref,
    send_one,
    recv_one,
    send_two,
    recv_two,
    edge_in,
    info_in,
    ghost_in,
    radial_ref,
    slope_ref,
    up_ref,
    m_ref,
    s_ref,
    hot_one,
    hot_two,
    hot_back,
    hot_ghost,
    g_wide,
    g_tall,
    s1,
    r1,
    s2,
    r2,
    load_sem,
    feats_ref,
    species_ref,
    export_ref,
    first_ref,
    second_ref,
    live_ref,
    disp_ref,
    w_up_ref,
    one_ref,
    two_ref,
    three_ref,
    power_ref,
    w_mix_ref,
    read_ref,
    base_ref,
):
    atoms, channels = feats_ref.shape
    pairs = first_ref.shape[1]
    slots = plan.slots
    head = pairs - 27 * slots
    cut = head // 128 * 128
    width = pairs - cut
    pad = head - cut
    orders = one_ref.shape[0]
    norm = 1.0 / math.sqrt(2.0 * pairs / atoms)

    me = tuple(lax.axis_index(a) for a in ("groups", "gx", "gy", "gz"))

    def device(d, turn):
        place = [me[0]]
        for here, step, n in zip(me[1:], plan.shift(d), plan.sizes):
            place.append(lax.rem(here + turn * step + n, n))
        return tuple(place)

    barrier = pltpu.get_barrier_semaphore()
    for d in plan.others:
        pl.semaphore_signal(barrier, inc=1, device_id=device(d, 1), device_id_type=MESH)

    order = (
        (first_far, first_ref),
        (second_far, second_ref),
        (feats_far, feats_ref),
        (disp_far, disp_ref),
        (live_far, live_ref),
        (export_far, export_ref),
        (one_far, one_ref),
        (two_far, two_ref),
        (three_far, three_ref),
        (w_up_far, w_up_ref),
        (w_mix_far, w_mix_ref),
        (species_far, species_ref),
        (power_far, power_ref),
        (read_far, read_ref),
        (base_far, base_ref),
    )
    loads = [
        pltpu.make_async_copy(far, near, load_sem.at[i]) for i, (far, near) in enumerate(order)
    ]
    for load in loads:
        load.start()

    lane = lax.broadcasted_iota(jnp.int32, (1, width), 1)
    block = jnp.maximum(lane - pad, 0) >> 4
    offsets = plan.lane_offsets(block)
    own_lane = jnp.logical_or(lane < pad, block == 13)
    lane_sub = plan.sub(offsets)
    ghost_base = plan.index(offsets, turned=True) * slots

    for load in loads[:6]:
        load.wait()
    first = first_ref[...]
    second = second_ref[...]
    live = live_ref[...].astype(F32)
    vx, vy, vz = disp_ref[0:1, :], disp_ref[1:2, :], disp_ref[2:3, :]

    atom_row = lax.broadcasted_iota(jnp.int32, (atoms, pairs), 0)
    hot_one[...] = (atom_row == first).astype(F32).astype(BF16)
    hot_two[...] = (atom_row == second).astype(F32).astype(BF16)
    export_hot = (
        (lax.broadcasted_iota(jnp.int32, (atoms, slots), 0) == export_ref[...])
        .astype(F32)
        .astype(BF16)
    )
    feats = feats_ref[...]

    window_slot = (second[:, cut:] - atoms) & (slots - 1)
    rows16 = []
    for v in (vx, vy, vz):
        piece = v[:, cut:]
        for _ in range(3):
            hi = rounded(piece)
            rows16.append(hi)
            piece = piece - hi
    rows16.append(live[:, cut:])
    rows16.append(window_slot.astype(F32))
    rows16.append(jnp.zeros((16 - len(rows16), width), F32))
    group16 = jnp.concatenate(rows16, axis=0)
    tall_group = lax.broadcasted_iota(jnp.int32, (128, width), 0) >> 4
    tiled = jnp.concatenate([group16] * 8, axis=0)
    info_rows = jnp.transpose(jnp.where(tall_group == lane_sub, tiled, 0.0))

    def transposed_dot(a, b):
        return nn(jnp.transpose(a.astype(F32)).astype(BF16), b)

    first_rows = transposed_dot(hot_one[:, cut:], feats).astype(BF16)
    offered = transposed_dot(
        jnp.concatenate([export_hot.astype(F32), jnp.zeros((atoms, 128 - slots), F32)], axis=1),
        feats,
    )[:slots].astype(BF16)
    for d in plan.others:
        at = plan.start[d]
        send_one[at : at + slots, :] = offered
        tile = None
        for g in plan.members[d]:
            part = info_rows[pad + slots * g : pad + slots * (g + 1), :]
            tile = part if tile is None else tile + part
            spot = plan.block_start[g]
            send_one[spot : spot + slots, :] = first_rows[pad + slots * g : pad + slots * (g + 1), :]
        send_one[at + slots : at + 2 * slots, :] = tile.astype(BF16)

    pl.semaphore_wait(barrier, len(plan.others))
    first_copies = []
    for d in plan.others:
        part = pl.ds(plan.start[d], plan.rows[d])
        copy = pltpu.make_async_remote_copy(
            src_ref=send_one.at[part],
            dst_ref=recv_one.at[part],
            send_sem=s1.at[d],
            recv_sem=r1.at[d],
            device_id=device(d, 1),
            device_id_type=MESH,
        )
        copy.start()
        first_copies.append(copy)

    for load in loads[6:]:
        load.wait()
    one = split_weights(one_ref[...])
    two = split_weights(two_ref[...])
    three = split_weights(three_ref[...])
    w_up = w_up_ref[...]
    w_up_t = flipped(w_up)
    w_mix = w_mix_ref[...]
    w_mix_t = flipped(w_mix)
    tables = jnp.transpose(
        jnp.concatenate(
            [
                power_ref[...],
                read_ref[...],
                jnp.zeros((128 - 3 - read_ref.shape[0], channels), F32),
            ],
            axis=0,
        )
    )
    up_t = nt(w_up_t, feats).astype(BF16)

    weight = live * norm
    edges = []

    def geometry(ax, ay, az, at):
        distance, inverse, n = direction(ax, ay, az)
        radial, slope = radial_network(distance, inverse, orders, one, two, three)
        lanes = ax.shape[1]
        radial_ref[:, at : at + lanes] = radial
        slope_ref[:, at : at + lanes] = slope
        return inverse, n

    def scaled_hot(hot, rows, at):
        lanes = hot.shape[1]
        for k in range(9):
            scale = jnp.broadcast_to(rows[k], (16, lanes)).astype(BF16)
            scale = jnp.concatenate([scale] * (atoms // 16), axis=0)
            s_ref[k * atoms : (k + 1) * atoms, at : at + lanes] = hot * scale

    def messages(radial_at, up, at):
        lanes = up.shape[1]
        up_ref[:, at : at + lanes] = up.astype(BF16)
        for l in range(3):
            here = slice(l * channels, (l + 1) * channels)
            m_ref[here, at : at + lanes] = (
                radial_ref[here, radial_at : radial_at + lanes] * up
            ).astype(BF16)

    inverse_a, n_a = [], []
    for at in (0, cut):
        part = slice(at, at + width) if at else slice(0, cut)
        inverse, n = geometry(vx[:, part], vy[:, part], vz[:, part], part.start)
        inverse_a.append(inverse)
        n_a.append(n)
        scaled_hot(hot_one[:, part], harmonic_rows(n, weight[:, part]), part.start)
    turned_low = tuple(-x for x in n_a[0])
    scaled_hot(hot_two[:, :cut], harmonic_rows(turned_low, weight[:, :cut]), pairs)
    messages(0, nn(up_t, hot_two[:, :cut]), 0)
    messages(0, nn(up_t, hot_one[:, :cut]), pairs)
    ghost_row = lax.broadcasted_iota(jnp.int32, (plan.count * slots, width), 0)
    ghost_at = jnp.where(own_lane, -1, ghost_base + window_slot)
    hot_ghost[...] = (ghost_row == ghost_at).astype(F32).astype(BF16)
    edge_in[...] = first_rows
    info_in[...] = jnp.zeros((width, 128), BF16)
    ghost_in[...] = jnp.zeros((plan.count * slots, channels), BF16)

    row = lax.broadcasted_iota(jnp.int32, (width, 128), 0)
    row_block = jnp.maximum(row - pad, 0) >> 4
    row_sub = plan.sub(plan.lane_offsets(row_block))
    column = lax.broadcasted_iota(jnp.int32, (width, 128), 1) >> 4
    mask_one = (column == row_sub).astype(F32).astype(BF16)
    mask_two = (column == row_sub + 1).astype(F32).astype(BF16)
    pick_row = lax.broadcasted_iota(jnp.int32, (16, 128), 0)
    pick_at = lax.broadcasted_iota(jnp.int32, (16, 128), 1) & 15
    pick = jnp.where(pick_at < 9, (pick_at * 11) >> 5, pick_at - 6) == pick_row
    pick = pick.astype(F32).astype(BF16)
    power = [tables[:, l : l + 1] for l in range(3)]
    species = species_ref[...]
    picker = (lax.broadcasted_iota(jnp.int32, (128, atoms), 0) == species + 3).astype(F32)
    read_rows = lax.dot_general(
        tables,
        picker,
        (((1,), (0,)), ((), ())),
        precision=lax.Precision.HIGHEST,
        preferred_element_type=F32,
    )
    base = jnp.zeros((1, atoms), F32)
    for s in range(read_ref.shape[0]):
        base = base + jnp.where(species == s, base_ref[s], 0.0)

    def amps_of(degree, start, stop):
        low, high = DEGREE_ROWS[degree]
        return nt(
            m_ref[degree * channels : (degree + 1) * channels, start:stop],
            s_ref[low * atoms : high * atoms, start:stop],
        )

    early = [amps_of(l, 0, cut) + amps_of(l, pairs, pairs + cut) for l in range(3)]

    for copy in first_copies:
        copy.wait_recv()
    for d in plan.others:
        at = plan.start[d]
        ghost_in[d * slots : (d + 1) * slots, :] = recv_one[at : at + slots, :]
        tile = recv_one[at + slots : at + 2 * slots, :]
        for g in plan.members[d]:
            spot = plan.block_start[g]
            here = slice(pad + slots * g, pad + slots * (g + 1))
            edge_in[here, :] = recv_one[spot : spot + slots, :]
            info_in[here, :] = tile

    info_own = info_in[...] * mask_one
    incoming = nt(pick, info_own)
    slot_in = incoming[4:5, :].astype(jnp.int32)
    slot_hot = (lax.broadcasted_iota(jnp.int32, (slots, width), 0) == slot_in).astype(F32)
    export_rows = jnp.broadcast_to(export_ref[...].astype(F32), (8, slots))
    target = nn(export_rows.astype(BF16), slot_hot.astype(BF16))[0:1, :].astype(jnp.int32)
    target = jnp.where(own_lane, second[:, cut:], target)
    weight_b = jnp.where(own_lane, live[:, cut:], incoming[3:4, :]) * norm
    back = []
    for i, v in enumerate((vx, vy, vz)):
        back.append(-jnp.where(own_lane, v[:, cut:], incoming[i : i + 1, :]))
    hot_b = (lax.broadcasted_iota(jnp.int32, (atoms, width), 0) == target).astype(F32)
    hot_b = hot_b.astype(BF16)
    hot_back[...] = hot_b
    inverse_b, n_b = geometry(*back, pairs)
    scaled_hot(hot_b, harmonic_rows(n_b, weight_b), pairs + cut)
    ghost_up = nt(w_up_t, ghost_in[...]).astype(BF16)
    messages(cut, nn(up_t, hot_two[:, cut:]) + nn(ghost_up, hot_ghost[...]), cut)
    messages(pairs, rounded(nt(w_up_t, edge_in[...])), pairs + cut)

    amps = []
    for l, (low, high) in enumerate(DEGREE_ROWS):
        sums = early[l] + amps_of(l, cut, pairs) + amps_of(l, pairs + cut, 2 * pairs)
        amps += [sums[:, i * atoms : (i + 1) * atoms] for i in range(high - low)]
    product = amps[0]
    for l, (low, high) in enumerate(DEGREE_ROWS):
        total = amps[low] * amps[low]
        for k in range(low + 1, high):
            total = total + amps[k] * amps[k]
        product = product + power[l] * total
    mixed = nn(w_mix_t, product.astype(BF16))
    sigmoid = jax.nn.sigmoid(mixed)
    energy_ref[...] = jnp.sum(mixed * sigmoid * read_rows, axis=0, keepdims=True) + base
    grad_mixed = (read_rows * sigmoid * (1.0 + mixed * (1.0 - sigmoid))).astype(BF16)
    grad_product = nn(w_mix, grad_mixed)
    for l, (low, high) in enumerate(DEGREE_ROWS):
        twice = grad_product * (2.0 * power[l])
        for k in range(low, high):
            value = twice * amps[k]
            if k == 0:
                value = value + grad_product
            value = value.astype(BF16)
            g_wide[:, k * atoms : (k + 1) * atoms] = value
            g_tall[k * channels : (k + 1) * channels, :] = value

    def backward(at, radial_at, hot, n, inverse, w):
        lanes = hot.shape[1]
        here = slice(at, at + lanes)
        there = slice(radial_at, radial_at + lanes)
        source, along = 0.0, 0.0
        for l, (low, high) in enumerate(DEGREE_ROWS):
            held = nn(g_wide[:, low * atoms : high * atoms], s_ref[low * atoms : high * atoms, here])
            part = slice(l * channels, (l + 1) * channels)
            source = source + radial_ref[part, there] * held
            along = along + slope_ref[part, there] * held
        along = jnp.sum(along * up_ref[:, here].astype(F32), axis=0, keepdims=True)
        p = [None]
        for k in range(1, 9):
            l = 1 if k < 4 else 2
            gathered = nn(g_tall[k * channels : (k + 1) * channels, :], hot)
            values = m_ref[l * channels : (l + 1) * channels, here].astype(F32)
            p.append(jnp.sum(gathered * values, axis=0, keepdims=True))
        x, y, z = n
        dx = S3 * p[1] + S15 * (z * p[4] + y * p[5] - x * p[8]) - S5 * x * p[6]
        dy = S3 * p[2] + S15 * (x * p[5] + z * p[7]) + 2.0 * S5 * y * p[6]
        dz = S3 * p[3] + S15 * (x * p[4] + y * p[7] + z * p[8]) - S5 * z * p[6]
        scale = w * inverse
        radial_part = along - scale * (x * dx + y * dy + z * dz)
        g = (
            scale * dx + x * radial_part,
            scale * dy + y * radial_part,
            scale * dz + z * radial_part,
        )
        hi = [rounded(v) for v in g]
        lo = [v - h for v, h in zip(g, hi)]
        fill = jnp.zeros((10, lanes), F32)
        return source, jnp.concatenate(list(g) + [jnp.zeros((13, lanes), F32)], axis=0), (
            jnp.concatenate(hi + lo + [fill], axis=0).astype(BF16)
        )

    source_a, _, split_a = backward(
        cut, cut, hot_one[:, cut:], n_a[1], inverse_a[1], weight[:, cut:]
    )
    source_b, force_b, split_b = backward(
        pairs + cut, pairs, hot_back[...], n_b, inverse_b, weight_b
    )
    source_a = source_a.astype(BF16)
    ghost_grad = nt(hot_ghost[...], source_a)
    ghost_force = -nt(
        hot_ghost[...],
        jnp.concatenate([split_a.astype(F32), jnp.zeros((112, width), F32)], axis=0).astype(BF16),
    )
    edge_grad = jnp.transpose(source_b).astype(BF16)
    tiled = jnp.concatenate([-force_b] * 8, axis=0)
    edge_force = jnp.transpose(jnp.where(tall_group == lane_sub + 1, tiled, 0.0))
    second_copies = []
    for d in plan.others:
        at = plan.start[d]
        ghost = slice(d * slots, (d + 1) * slots)
        send_two[at : at + slots, :] = ghost_grad[ghost, :].astype(BF16)
        tile = ghost_force[ghost, :]
        for g in plan.members[d]:
            here = slice(pad + slots * g, pad + slots * (g + 1))
            tile = tile + edge_force[here, :]
            spot = plan.block_start[g]
            send_two[spot : spot + slots, :] = edge_grad[here, :]
        send_two[at + slots : at + 2 * slots, :] = tile.astype(BF16)
        part = pl.ds(at, plan.rows[d])
        copy = pltpu.make_async_remote_copy(
            src_ref=send_two.at[part],
            dst_ref=recv_two.at[part],
            send_sem=s2.at[d],
            recv_sem=r2.at[d],
            device_id=device(d, -1),
            device_id_type=MESH,
        )
        copy.start()
        second_copies.append(copy)

    source_c, _, split_c = backward(0, 0, hot_one[:, :cut], n_a[0], inverse_a[0], weight[:, :cut])
    source_d, _, split_d = backward(
        pairs, 0, hot_two[:, :cut], turned_low, inverse_a[0], weight[:, :cut]
    )
    grad_up = (
        nt(hot_two[:, cut:], source_a)
        + nt(hot_two[:, :cut], source_c.astype(BF16))
        + nt(hot_one[:, :cut], source_d.astype(BF16))
    )
    force = nt(split_a, hot_one[:, cut:]) - nt(split_a, hot_two[:, cut:])
    force = force + nt(split_b, hot_back[...])
    force = force + nt(split_c, hot_one[:, :cut]) - nt(split_c, hot_two[:, :cut])
    force = force + nt(split_d, hot_two[:, :cut]) - nt(split_d, hot_one[:, :cut])
    edge_in[...] = edge_grad
    info_in[...] = edge_force.astype(BF16)

    for copy in second_copies:
        copy.wait_recv()
    offered_grad, offered_force = 0.0, 0.0
    for d in plan.others:
        at = plan.start[d]
        offered_grad = offered_grad + recv_two[at : at + slots, :].astype(F32)
        tile = recv_two[at + slots : at + 2 * slots, :]
        offered_force = offered_force + tile.astype(F32)
        for g in plan.members[d]:
            spot = plan.block_start[g]
            here = slice(pad + slots * g, pad + slots * (g + 1))
            edge_in[here, :] = recv_two[spot : spot + slots, :]
            info_in[here, :] = tile
    info_own = info_in[...] * mask_two
    offered_column = lax.broadcasted_iota(jnp.int32, (slots, 128), 1)
    offered_force = jnp.where(offered_column < 16, offered_force, 0.0)
    window_hot = hot_one[:, cut:]
    grad_up = grad_up + nn(window_hot, edge_in[...]) + nn(export_hot, offered_grad.astype(BF16))
    remote_force = nn(window_hot, info_own) + nn(export_hot, offered_force.astype(BF16))
    remote_force = jnp.transpose(remote_force)
    total = force[0:3, :] + force[3:6, :]
    for j in range(8):
        total = total + remote_force[16 * j : 16 * j + 3, :] + remote_force[16 * j + 3 : 16 * j + 6, :]
    for copy in first_copies + second_copies:
        copy.wait_send()
    force_ref[...] = total
    grad_ref[...] = nt(grad_up.astype(BF16), w_up).astype(BF16)


def place(a_ref, b_ref, c_ref, a_out, b_out, c_out, sem):
    pairs = ((a_ref, a_out), (b_ref, b_out), (c_ref, c_out))
    copies = [pltpu.make_async_copy(a, b, sem.at[i]) for i, (a, b) in enumerate(pairs)]
    for copy in copies:
        copy.start()
    for copy in copies:
        copy.wait()


def on_device(plan, *args):
    (
        node_feats,
        species,
        export_index,
        pair_first,
        pair_second,
        pair_live,
        displacement,
        w_up,
        radial_one,
        radial_two,
        radial_three,
        power_weight,
        w_mix,
        read_table,
        base_energy,
    ) = args
    atoms, channels = node_feats.shape
    pairs = pair_first.shape[0]
    slots = export_index.shape[0]
    cut = (pairs - 27 * slots) // 128 * 128
    width = pairs - cut
    ghosts = plan.count * slots
    vmem = pl.BlockSpec(memory_space=pltpu.VMEM)
    operands = (
        node_feats,
        species.reshape(1, atoms),
        export_index.reshape(1, slots),
        pair_first.reshape(1, pairs),
        pair_second.reshape(1, pairs),
        pair_live.reshape(1, pairs),
        displacement,
        w_up,
        radial_one,
        radial_two,
        radial_three,
        power_weight,
        w_mix,
        read_table,
        base_energy,
    )
    energy, forces, grad = pl.pallas_call(
        functools.partial(kernel, plan),
        out_shape=(
            jax.ShapeDtypeStruct((1, atoms), F32),
            jax.ShapeDtypeStruct((3, atoms), F32),
            jax.ShapeDtypeStruct((atoms, channels), BF16),
        ),
        in_specs=[pl.BlockSpec(memory_space=pltpu.HBM)] * 15,
        out_specs=(vmem,) * 3,
        scratch_shapes=[pltpu.VMEM((plan.total, channels), BF16)] * 4
        + [
            pltpu.VMEM((width, channels), BF16),
            pltpu.VMEM((width, 128), BF16),
            pltpu.VMEM((ghosts, channels), BF16),
            pltpu.VMEM((3 * channels, pairs + width), F32),
            pltpu.VMEM((3 * channels, pairs + width), F32),
            pltpu.VMEM((channels, 2 * pairs), BF16),
            pltpu.VMEM((3 * channels, 2 * pairs), BF16),
            pltpu.VMEM((9 * atoms, 2 * pairs), BF16),
            pltpu.VMEM((atoms, pairs), BF16),
            pltpu.VMEM((atoms, pairs), BF16),
            pltpu.VMEM((atoms, width), BF16),
            pltpu.VMEM((ghosts, width), BF16),
            pltpu.VMEM((channels, 9 * atoms), BF16),
            pltpu.VMEM((9 * channels, atoms), BF16),
        ]
        + [pltpu.SemaphoreType.DMA((plan.count,))] * 4
        + [pltpu.SemaphoreType.DMA((len(operands),))]
        + [pltpu.VMEM(v.shape, v.dtype) for v in operands[:-1]]
        + [pltpu.SMEM(base_energy.shape, F32)],
        compiler_params=pltpu.CompilerParams(
            collective_id=0, has_side_effects=True, vmem_limit_bytes=64 * 1024 * 1024
        ),
    )(*operands)
    results = (energy, forces, grad)
    energy, forces, grad = pl.pallas_call(
        place,
        out_shape=tuple(jax.ShapeDtypeStruct(v.shape, v.dtype) for v in results),
        in_specs=[vmem] * 3,
        out_specs=(pl.BlockSpec(memory_space=pl.ANY),) * 3,
        scratch_shapes=[pltpu.SemaphoreType.DMA((3,))],
        compiler_params=pltpu.CompilerParams(has_side_effects=True),
    )(*results)
    return energy.reshape(atoms), forces, grad


def solution(mesh):
    every = ("groups", "gx", "gy", "gz")
    plan = Plan(tuple(mesh.shape[a] for a in ("gx", "gy", "gz")), 16)
    in_specs = (
        (P(every, None),) + (P(every),) * 5 + (P(None, every),) + (P(),) * 8
    )
    out_specs = (P(every), P(None, every), P(every, None))
    return jax.shard_map(
        functools.partial(on_device, plan),
        mesh=mesh,
        in_specs=in_specs,
        out_specs=out_specs,
        check_vma=False,
    )
```
